256 devices in a mesh: fsdp: 64 (over z, x, core), tp: 4 (over y).
Axes of the slice: x: 4, y: 4, z: 8, core: 2. Of those that a mesh axis runs over, the one named last changes fastest.
Arguments:
- tokens: bfloat16 [4096, 3072], P('fsdp', 'tp'), may hold values from -6 to 6
- cotangent: bfloat16 [4096, 3072], P('fsdp', 'tp'), may hold values from -0.52734375 to 0.52734375
- expert_ids: int32 [4096, 2], P('fsdp'), may hold values from 0 to 3, all different within a row; in each aligned block of 64 rows (0 to 63, 64 to 127, ...) at most 36 rows name the same one
- route_weights: float32 [4096, 2], P('fsdp'), may hold values from 0.2 to 1
- gate_weight: bfloat16 [3072, 32768], P('tp', 'fsdp'), may hold values from -0.109375 to 0.109375
- up_weight: bfloat16 [3072, 32768], P('tp', 'fsdp'), may hold values from -0.109375 to 0.109375
- down_weight: bfloat16 [32768, 3072], P('fsdp', 'tp'), may hold values from -0.0625 to 0.0625
- projector: bfloat16 [4, 3072, 512], P(None, 'tp'), may hold values from -0.109375 to 0.109375
- first_moment: float32 [32768, 512], P('fsdp'), may hold values from -3 to 3
- second_moment: float32 [32768, 512], P('fsdp'), may hold values from 0.05 to 1
Outputs:
- mixed: bfloat16 [4096, 3072], P('fsdp', 'tp')
- down_update: float32 [32768, 3072], P('fsdp', 'tp')
- new_first: float32 [32768, 512], P('fsdp')
- new_second: float32 [32768, 512], P('fsdp')
The draws below stay inside these ranges and needn't reach their ends.
Inputs may be any that keep to these rules, and one draw needn't show every extreme that they name: `expert_ids`: the two ids of a token differ. In each aligned block of 64 tokens (the tokens of one index of fsdp) no expert is named by more than 36 tokens, a bound that some block reaches.
All inputs are finite; a program needn't handle non-finite values.
Results may differ from the reference program's by a relative error of at most 0.022.
Values may be sent and summed in bfloat16 or wider, within the bound.
A program may use at most 128 MiB of HBM per device.

```python
import math
import jax
import jax.numpy as jnp
import numpy as np
from jax import lax

D = 3072
FF = 8192
EXPERTS = 4
RANK = 512
TOK_DEV = 64
MOST = 36
TOKENS = 4096
N_FSDP = 64


def shard_levels(stream_key, shape, split, least, top_value):
    gain, own = 1.0, jax.random.fold_in(stream_key, 6)
    for dim, parts in split:
        heights = jnp.exp(jax.random.uniform(jax.random.fold_in(own, dim), (parts,), jnp.float32, least / len(split), top_value / len(split)))
        gain = gain * jnp.repeat(heights, shape[dim] // parts).reshape([-1 if axis == dim else 1 for axis in range(len(shape))])
    return gain


def assign_block(rng, own, number, rows, amount, top, reach, lean):
    ranking = jax.random.permutation(rng, amount)
    heavy_load, usual = shares(amount, rows * top, reach, lean, True), shares(amount, rows * top, reach, lean, False)
    places = jnp.arange(amount)

    def named(sizes, offset_by):
        used = int((sizes > 0).sum())
        fixed = max(1, used // 4)
        shifted = fixed + (places - fixed + offset_by * (used - fixed)) % max(1, amount - fixed)
        return jnp.zeros((amount,), jnp.int32).at[ranking[jnp.where(places < fixed, places, shifted)]].set(jnp.asarray(sizes, jnp.int32))

    sizes = jnp.where(number % 4 == 0, named(heavy_load, number // 4), named(usual, number - number // 4 - 1))
    mixed = jax.random.permutation(jax.random.fold_in(own, 3), amount)
    source_of, sink = mixed[0:amount // 2 * 2:2], mixed[1:amount // 2 * 2:2]
    slack = jnp.minimum(sizes[source_of] - 1, reach - sizes[sink]) // 2
    slack = jnp.where((source_of == ranking[0]) | (sink == ranking[0]) | (sizes[sink] == 0), 0, jnp.maximum(slack, 0))
    shifted = jax.random.randint(jax.random.fold_in(own, 4), (amount // 2,), 0, 1 << 20) % (slack + 1)
    sizes = sizes.at[source_of].add(-shifted).at[sink].add(shifted)
    labels = jnp.searchsorted(jnp.cumsum(sizes), jnp.arange(rows * top), side="right").astype(jnp.int32)
    listing = labels.reshape(top, rows).T
    listing = listing[jax.random.permutation(jax.random.fold_in(own, 1), rows)]
    offset_by = jax.random.randint(jax.random.fold_in(own, 2), (rows, 1), 0, top)
    return jnp.take_along_axis(listing, (jnp.arange(top)[None, :] + offset_by) % top, axis=1)


def shares(count, total, reach, lean, full):
    portions = [(1 << 20) // math.isqrt(grade ** lean) + 1 for grade in range(1, count + 1)]
    largest = reach if full else min(reach, max(-(-total // count), total * portions[0] // sum(portions)))
    least = 1 if total - largest >= count - 1 else 0
    given, rest = [largest] + [least] * (count - 1), total - largest - least * (count - 1)
    while rest > 0:
        movable = [i for i in range(1, count) if given[i] < largest] or [i for i in range(1, count) if given[i] < reach]
        pool, budget = sum([portions[i] for i in movable]), rest
        for i in movable:
            extra = min(reach - given[i], max(1, budget * portions[i] // pool), rest)
            given[i] = given[i] + extra
            rest = rest - extra
    return np.array(given)


def normal_values(rng, shape, spread, reach, shards=(), kind=jnp.bfloat16):
    values = spread * jax.random.normal(rng, shape, jnp.float32)
    if shards:
        values = values * shard_levels(rng, shape, shards, -0.22, 0.18)
    return jnp.clip(values, -reach, reach).astype(kind)


def setup_inputs(seed: int = 0) -> dict:
    key_list = jax.random.split(jax.random.key(seed), 11)
    tokens = normal_values(key_list[0], (TOKENS, D), 1.0, 6.0, ((0, 64), (1, 4)))
    cotangent = normal_values(key_list[1], (TOKENS, D), (4.0 / (N_FSDP * TOK_DEV // 2) ** 0.5), 0.52734375, ((0, 64), (1, 4)))
    expert_ids_keys = jax.random.split(jax.random.fold_in(key_list[2], 1), TOKENS // TOK_DEV)
    expert_ids_turns = jax.random.permutation(jax.random.fold_in(key_list[2], 3), TOKENS // TOK_DEV)
    expert_ids = jax.vmap(lambda own, number: assign_block(jax.random.fold_in(key_list[2], 2), own, number, TOK_DEV, EXPERTS, 2, MOST, 1))(expert_ids_keys, expert_ids_turns).reshape((TOKENS, 2))
    route_weights = jnp.clip(0.2 + 0.8 * jax.random.uniform(key_list[3], (TOKENS, 2), jnp.float32) ** shard_levels(key_list[3], (TOKENS, 2), ((0, 64),), -0.2, 0.2), 0.2, 1.0)
    gate_weight = normal_values(key_list[4], (D, EXPERTS * FF), D ** -0.5, 0.109375, ((0, 4), (1, 64)))
    up_weight = normal_values(key_list[5], (D, EXPERTS * FF), D ** -0.5, 0.109375, ((0, 4), (1, 64)))
    down_weight = normal_values(key_list[6], (EXPERTS * FF, D), FF ** -0.5, 0.0625, ((0, 64), (1, 4)))
    projector = normal_values(key_list[7], (EXPERTS, D, RANK), D ** -0.5, 0.109375, ((1, 4),))
    first_moment = normal_values(key_list[8], (EXPERTS * FF, RANK), 0.5, 3.0, ((0, 64),), jnp.float32)
    second_moment = jnp.clip(jnp.exp(math.log(1.0) - 2.9957323 * jax.random.uniform(key_list[9], (EXPERTS * FF, RANK), jnp.float32) ** shard_levels(key_list[9], (EXPERTS * FF, RANK), ((0, 64),), -0.2, 0.2)), 0.05, 1.0)
    return dict(tokens=tokens, cotangent=cotangent, expert_ids=expert_ids, route_weights=route_weights, gate_weight=gate_weight, up_weight=up_weight, down_weight=down_weight, projector=projector, first_moment=first_moment, second_moment=second_moment)


def slot_positions(expert_ids):
    blocks = expert_ids.reshape(N_FSDP, TOK_DEV, 2)
    onehot = (blocks[:, :, :, None] == jnp.arange(EXPERTS, dtype=jnp.int32)[None, None, None, :]).astype(jnp.int32)
    per_token = lax.optimization_barrier(jnp.sum(onehot, axis=2))
    before = jnp.cumsum(per_token, axis=1) - per_token
    return lax.optimization_barrier(jnp.sum(onehot * before[:, :, None, :], axis=3)).astype(jnp.int32)

def reference(tokens, cotangent, expert_ids, route_weights, gate_weight, up_weight, down_weight, projector, first_moment, second_moment):
    blocks = expert_ids.reshape(N_FSDP, TOK_DEV, 2)
    position = slot_positions(expert_ids)
    weights = route_weights.reshape(N_FSDP, TOK_DEV, 2)
    source = jnp.broadcast_to(jnp.arange(N_FSDP, dtype=jnp.int32)[:, None, None], (N_FSDP, TOK_DEV, 2))
    local = jnp.broadcast_to(jnp.arange(TOK_DEV, dtype=jnp.int32)[None, :, None], (N_FSDP, TOK_DEV, 2))
    slot_id = (blocks * MOST + position).astype(jnp.int32)
    table = jnp.full((N_FSDP, EXPERTS * MOST), TOK_DEV, jnp.int32).at[source, slot_id].set(local)
    slot_weight = jnp.zeros((N_FSDP, EXPERTS * MOST), jnp.float32).at[source, slot_id].set(weights)
    pad_rows = jnp.zeros((N_FSDP, 1, D), jnp.bfloat16)
    token_pad = jnp.concatenate([tokens.reshape(N_FSDP, TOK_DEV, D), pad_rows], axis=1)
    grad_pad = jnp.concatenate([cotangent.reshape(N_FSDP, TOK_DEV, D), pad_rows], axis=1)
    routed = jnp.take_along_axis(token_pad, table[:, :, None], axis=1)
    routed_grad = jnp.take_along_axis(grad_pad, table[:, :, None], axis=1)
    scaled = (routed_grad.astype(jnp.float32) * slot_weight[:, :, None]).astype(jnp.bfloat16)
    outputs = []
    updates = []
    firsts = []
    seconds = []
    bias_one = 1.0 - 0.9 ** 10
    bias_two = 1.0 - 0.999 ** 10
    for expert in range(EXPERTS):
        rows = routed[:, expert * MOST:(expert + 1) * MOST].reshape(N_FSDP * MOST, D)
        rows_grad = scaled[:, expert * MOST:(expert + 1) * MOST].reshape(N_FSDP * MOST, D)
        gate = jnp.dot(rows, gate_weight[:, expert * FF:(expert + 1) * FF], preferred_element_type=jnp.float32)
        upper = jnp.dot(rows, up_weight[:, expert * FF:(expert + 1) * FF], preferred_element_type=jnp.float32)
        hidden = (jax.nn.silu(gate) * upper).astype(jnp.bfloat16)
        outputs.append(jnp.dot(hidden, down_weight[expert * FF:(expert + 1) * FF], preferred_element_type=jnp.float32))
        grad = lax.dot_general(hidden, rows_grad, (((0,), (0,)), ((), ())), preferred_element_type=jnp.float32)
        basis = projector[expert].astype(jnp.float32)
        low = jnp.dot(grad, basis, precision=lax.Precision.HIGHEST)
        first = 0.9 * first_moment[expert * FF:(expert + 1) * FF] + 0.1 * low
        second = 0.999 * second_moment[expert * FF:(expert + 1) * FF] + 0.001 * low * low
        direction = first / bias_one / (jnp.sqrt(second / bias_two) + 1e-08)
        updates.append(jnp.dot(direction, basis.T, precision=lax.Precision.HIGHEST))
        firsts.append(first)
        seconds.append(second)
    stacked = jnp.concatenate(outputs, axis=0)
    mixed = jnp.zeros((N_FSDP, TOK_DEV, D), jnp.float32)
    for which in range(2):
        index = (blocks[:, :, which] * (N_FSDP * MOST) + jnp.arange(N_FSDP, dtype=jnp.int32)[:, None] * MOST + position[:, :, which]).astype(jnp.int32)
        mixed = mixed + weights[:, :, which][:, :, None] * stacked[index]
    mixed = mixed.reshape(TOKENS, D).astype(jnp.bfloat16)
    return (mixed, jnp.concatenate(updates, axis=0), jnp.concatenate(firsts, axis=0), jnp.concatenate(seconds, axis=0))
```

```python
import functools

import jax
import jax.numpy as jnp
from jax import lax
from jax.experimental import pallas as pl
from jax.experimental.pallas import tpu as pltpu
from jax.sharding import PartitionSpec as P

EXPERTS = 4
MOST = 36
PAD = 48
ROWS = 4 * MOST
PIECES = 8
RELZ = (0, 1, -1, 2, -2, 3, -3, 4)
LAG1, LAG2, LAG3, LAG4 = 1, 2, 3, 4
MESH = pl.DeviceIdType.MESH
F32, BF16 = jnp.float32, jnp.bfloat16


def dot(a, b):
    return jnp.dot(a, b, preferred_element_type=F32)


def dot_t(a, b):
    return lax.dot_general(a, b, (((0,), (0,)), ((), ())), preferred_element_type=F32)


def moe_kernel(
    ids_ref, route_ref, tok_ref, cot_ref, wg_hbm, wu_hbm, wd_hbm, proj_hbm,
    mixed_ref, low_ref,
    wg, wu, wd, proj, pick_s, slotw_s, xs, sps, spr, spz, zb, zs, xb, spb,
    p2, pr, pll, qa, po, ra, rb, fl, fr, hd, out, cb, eb, rbk, lowt, lc, lr, lo,
    lsem, wsend, wrecv, zsend, zrecv, zssend, zsrecv, sysend, syrecv, sxsend, sxrecv,
    xsend, xrecv, xfsend, xfrecv, ysend, yrecv, csend, crecv, rsend, rrecv, lcsend, lcrecv, losend, lorecv,
):
    f = lax.axis_index("fsdp")
    y = lax.axis_index("tp")
    z, x, c = f // 8, (f // 2) % 4, f % 2
    yr, yl, yo = (y + 1) % 4, (y + 3) % 4, (y + 2) % 4

    def at_y(yy):
        return (f, yy)

    def at_x(step):
        return (z * 8 + ((x + step) % 4) * 2 + c, y)

    def at_z(zz):
        return (zz * 8 + x * 2 + c, y)

    sibling = (z * 8 + x * 2 + (1 - c), y)

    def rcopy(src, dst, send, recv, dev):
        return pltpu.make_async_remote_copy(
            src_ref=src, dst_ref=dst, send_sem=send, recv_sem=recv, device_id=dev, device_id_type=MESH
        )

    local = []
    for k in range(2):
        cols = pl.ds(k * 256, 256)
        local.append(pltpu.make_async_copy(wg_hbm.at[:, cols], wg.at[2 * c + k], lsem.at[k]))
        local.append(pltpu.make_async_copy(wu_hbm.at[:, cols], wu.at[2 * c + k], lsem.at[2 + k]))
    local.append(pltpu.make_async_copy(wd_hbm, wd.at[c], lsem.at[4]))
    local.append(pltpu.make_async_copy(proj_hbm, proj, lsem.at[5]))
    for cp in local:
        cp.start()

    barrier = pltpu.get_barrier_semaphore()
    partners = [at_y(yr), at_y(yl), at_y(yo), at_x(1), at_x(3), at_x(2), sibling]
    partners += [at_z((z + k) % 8) for k in range(1, 8)]
    for dev in partners:
        pl.semaphore_signal(barrier, inc=1, device_id=dev, device_id_type=MESH)

    slot = lax.broadcasted_iota(jnp.int32, (EXPERTS * PAD, 64), 0)
    slot_e = (slot >= PAD).astype(jnp.int32) + (slot >= 2 * PAD).astype(jnp.int32) + (slot >= 3 * PAD).astype(jnp.int32)
    slot_j = slot - PAD * slot_e
    named0 = (ids_ref[0:1, :] == slot_e).astype(F32)
    named1 = (ids_ref[1:2, :] == slot_e).astype(F32)
    named = named0 + named1
    earlier = (
        lax.broadcasted_iota(jnp.int32, (64, 64), 0) < lax.broadcasted_iota(jnp.int32, (64, 64), 1)
    ).astype(F32)
    before = dot(named.astype(BF16), earlier.astype(BF16))
    pick = jnp.where(before == slot_j.astype(F32), named, 0.0)
    slot_w = jnp.sum(pick * (named0 * route_ref[0:1, :] + named1 * route_ref[1:2, :]), axis=1, keepdims=True)
    pick = pick.astype(BF16)
    pick_s[...] = pick
    slotw_s[...] = slot_w
    rows = dot(pick, tok_ref[...]).astype(BF16)
    xs[...] = rows.reshape(EXPERTS, PAD, 768)

    pl.semaphore_wait(barrier, len(partners))

    remote = []
    for k in range(2):
        cols = pl.ds(k * 256, 256)
        remote.append((wg_hbm.at[:, cols], wg, 2 * c + k, 2 * (1 - c) + k))
        remote.append((wu_hbm.at[:, cols], wu, 2 * c + k, 2 * (1 - c) + k))
    remote.append((wd_hbm, wd, c, 1 - c))
    wcopies = [rcopy(s, d.at[mine], wsend.at[n], wrecv.at[n], sibling) for n, (s, d, mine, _) in enumerate(remote)]
    wwaits = [rcopy(s, d.at[theirs], wsend.at[n], wrecv.at[n], sibling) for n, (s, d, _, theirs) in enumerate(remote)]

    def zcopy(k):
        there = (z + 8 - RELZ[k]) % 8
        return rcopy(xs.at[there // 2], zb.at[k // 4, k % 4], zsend.at[k], zrecv.at[k], at_z(there))

    def zscopy(k):
        there = (z + 8 - RELZ[k]) % 8
        return rcopy(spz.at[there // 2], zs.at[k // 4, k % 4], zssend.at[k], zsrecv.at[k], at_z(there))

    for k in range(1, 8):
        zcopy(k).start()
    for cp in wcopies:
        cp.start()
    zb[0, 0] = xs[z // 2]

    local[5].wait()
    scaled = (dot(pick, cot_ref[...]) * slot_w).astype(BF16)
    for e in range(EXPERTS):
        part = dot(scaled[e * PAD:(e + 1) * PAD], proj[e]).astype(BF16)
        for d in range(4):
            sps[d, e * PAD:(e + 1) * PAD, :] = part[:, d * 128:(d + 1) * 128]
    sycopies = [
        rcopy(sps.at[d], spr.at[k], sysend.at[k], syrecv.at[k], at_y(d)) for k, d in enumerate((yr, yl, yo))
    ]
    for cp in sycopies:
        cp.start()

    def squeeze():
        r = lax.broadcasted_iota(jnp.int32, (ROWS, 4 * PAD), 0)
        col = lax.broadcasted_iota(jnp.int32, (ROWS, 4 * PAD), 1)
        src = (r >= MOST).astype(jnp.int32) + (r >= 2 * MOST).astype(jnp.int32) + (r >= 3 * MOST).astype(jnp.int32)
        return (col == r + (PAD - MOST) * src).astype(F32).astype(BF16)

    def widen():
        r = lax.broadcasted_iota(jnp.int32, (4 * PAD, ROWS), 1)
        col = lax.broadcasted_iota(jnp.int32, (4 * PAD, ROWS), 0)
        src = (r >= MOST).astype(jnp.int32) + (r >= 2 * MOST).astype(jnp.int32) + (r >= 3 * MOST).astype(jnp.int32)
        return (col == r + (PAD - MOST) * src).astype(F32).astype(BF16)

    def xcopy(h, r):
        return rcopy(xb.at[4 * h], xb.at[4 * h + r], xsend.at[4 * h + r], xrecv.at[4 * h + r], at_x(1 if r == 2 else 3))

    def xforward(h, r):
        if r == 2:
            return rcopy(xb.at[4 * h + 2, 0], xb.at[4 * h + 3, 0], xfsend.at[h, 0], xfrecv.at[h, 0], at_x(1))
        return rcopy(xb.at[4 * h + 1, 1], xb.at[4 * h + 3, 1], xfsend.at[h, 1], xfrecv.at[h, 1], at_x(3))

    def gather_rows(h):
        for k in range(4 * h, 4 * h + 4):
            if k:
                zcopy(k).wait_recv()
        dense = dot(squeeze(), zb[h].reshape(4 * PAD, 768)).astype(BF16)
        xb[4 * h, 0] = dense[:, :384]
        xb[4 * h, 1] = dense[:, 384:]
        xcopy(h, 2).start()
        xcopy(h, 1).start()

    def sxcopy(k):
        return rcopy(spb.at[0], spb.at[(2, 1, 3)[k]], sxsend.at[k], sxrecv.at[k], at_x((1, 3, 2)[k]))

    gather_rows(0)
    for cp in local[:5]:
        cp.wait()
    for cp in wwaits[:4]:
        cp.wait_recv()

    def ycopy(kind, i):
        src, dst, dev = {
            0: lambda: (p2.at[i, 0], ra.at[i], yr),
            1: lambda: (p2.at[i, 1], rb.at[i], yl),
            2: lambda: (pr.at[i, 1], fl.at[i, 1], yr),
            3: lambda: (pll.at[i, 0], fr.at[i, 0], yl),
            4: lambda: (pr.at[i, 0], fl.at[i, 0], yr),
            5: lambda: (pll.at[i, 1], fr.at[i, 1], yl),
            6: lambda: (hd.at[i, y], hd.at[i, y], yr),
            7: lambda: (hd.at[i, y], hd.at[i, y], yl),
            8: lambda: (hd.at[i, yl, 0], hd.at[i, yl, 0], yr),
            9: lambda: (hd.at[i, yr, 1], hd.at[i, yr, 1], yl),
        }[kind]()
        return rcopy(src, dst, ysend.at[kind, i], yrecv.at[kind, i], at_y(dev))

    def yarrive(kind, i):
        if kind < 6:
            ycopy(kind, i).wait_recv()
            return
        dst = {
            6: lambda: hd.at[i, yl],
            7: lambda: hd.at[i, yr],
            8: lambda: hd.at[i, yo, 0],
            9: lambda: hd.at[i, yo, 1],
        }[kind]()
        rcopy(dst, dst, ysend.at[kind, i], yrecv.at[kind, i], at_y(yr)).wait_recv()

    def stage0(i):
        h, r = i // 4, i % 4

        @pl.when(r == 1)
        def _():
            xcopy_wait(i)
            xforward(h, 1).start()

        @pl.when(r == 2)
        def _():
            xcopy_wait(i)
            xforward(h, 2).start()

        @pl.when(r == 3)
        def _():
            xforward(h, 2).wait_recv()
            xforward(h, 1).wait_recv()

        v = jnp.concatenate([xb[i, 0], xb[i, 1]], axis=1)
        p2[i, 0] = dot(v, wg[yo]).astype(BF16)
        ycopy(0, i).start()
        p2[i, 1] = dot(v, wu[yo]).astype(BF16)
        ycopy(1, i).start()
        pr[i, 1] = dot(v, wu[yr]).astype(BF16)
        ycopy(2, i).start()
        pll[i, 0] = dot(v, wg[yl]).astype(BF16)
        ycopy(3, i).start()
        qa[i, 0] = dot(v, wg[yr])
        qa[i, 1] = dot(v, wu[yl])
        po[i, 0] = dot(v, wg[y])
        po[i, 1] = dot(v, wu[y])

    def xcopy_wait(i):
        rcopy(xb.at[i], xb.at[i], xsend.at[i], xrecv.at[i], at_x(1)).wait_recv()

    def stage1(i):
        yarrive(0, i)
        pr[i, 0] = (qa[i, 0] + ra[i].astype(F32)).astype(BF16)
        ycopy(4, i).start()
        yarrive(1, i)
        pll[i, 1] = (qa[i, 1] + rb[i].astype(F32)).astype(BF16)
        ycopy(5, i).start()

    def stage2(i):
        for kind in (2, 3, 4, 5):
            yarrive(kind, i)
        g = po[i, 0] + fl[i, 0].astype(F32) + fr[i, 0].astype(F32)
        u = po[i, 1] + fl[i, 1].astype(F32) + fr[i, 1].astype(F32)
        hidden = (g / (1.0 + jnp.exp(-g)) * u).astype(BF16)
        hd[i, y, 0] = hidden[:, :128]
        hd[i, y, 1] = hidden[:, 128:]
        ycopy(6, i).start()
        ycopy(7, i).start()

    def stage3(i):
        yarrive(6, i)
        ycopy(8, i).start()
        yarrive(7, i)
        ycopy(9, i).start()

    def ccopy(i):
        h, r = i // 4, i % 4
        step = jnp.where(r == 1, 1, jnp.where(r == 2, 3, 2))
        there = 4 * h + jnp.where(r == 3, 3, 3 - r)
        return rcopy(out.at[i], cb.at[there], csend.at[i], crecv.at[there], at_x(step))

    def carrive(i):
        return rcopy(cb.at[i], cb.at[i], csend.at[i], crecv.at[i], at_x(1))

    def stage4(i):
        h, r = i // 4, i % 4
        yarrive(8, i)
        yarrive(9, i)
        hidden = jnp.concatenate([hd[i, d, k] for d in range(4) for k in range(2)], axis=1)
        out[i] = dot(hidden, wd[...].reshape(1024, 768)).astype(BF16)

        @pl.when(r > 0)
        def _():
            ccopy(i).start()

        lowt[...] += dot_t(spb[r, h], hidden)

    def rcopy_back(k):
        there = (z + 8 + RELZ[k]) % 8
        return rcopy(eb.at[k // 4, k % 4], rbk.at[z % 2, z // 2], rsend.at[k], rrecv.at[k], at_z(there))

    def rarrive(k):
        come = (z + 8 - RELZ[k]) % 8
        dst = rbk.at[come % 2, come // 2]
        return rcopy(dst, dst, rsend.at[k], rrecv.at[k], at_z((z + 1) % 8))

    def combine(h):
        for r in range(1, 4):
            carrive(4 * h + r).wait_recv()
        total = out[4 * h].astype(F32)
        for r in range(1, 4):
            total = total + cb[4 * h + r].astype(F32)
        wide = dot(widen(), total.astype(BF16)).astype(BF16)
        eb[h] = wide.reshape(4, PAD, 768)
        for k in range(4 * h, 4 * h + 4):
            if k:
                rcopy_back(k).start()
            else:
                rbk[z % 2, z // 2] = eb[0, 0]

    lowt[...] = jnp.zeros_like(lowt)

    def step(it, carry):
        @pl.when(it == 1)
        def _():
            for cp in sycopies:
                cp.wait_recv()
            total = sps[y].astype(F32)
            for k in range(3):
                total = total + spr[k].astype(F32)
            spz[...] = total.astype(BF16).reshape(EXPERTS, PAD, 128)
            for k in range(1, 8):
                zscopy(k).start()
            zs[0, 0] = spz[z // 2]

        @pl.when(it == 2)
        def _():
            gather_rows(1)

        @pl.when(it == 3)
        def _():
            for k in range(1, 8):
                zscopy(k).wait_recv()
            for h in range(2):
                spb[0, h] = dot(squeeze(), zs[h].reshape(4 * PAD, 128)).astype(BF16)
            for k in range(3):
                sxcopy(k).start()

        def run(stage, lag):
            @pl.when((it >= lag) & (it < lag + PIECES))
            def _():
                stage(it - lag)

        run(stage3, LAG3)
        run(stage2, LAG2)
        run(stage1, LAG1)
        run(stage0, 0)

        @pl.when(it == LAG4)
        def _():
            for k in range(3):
                sxcopy(k).wait_recv()
            wwaits[4].wait_recv()

        run(stage4, LAG4)

        @pl.when(it == LAG4 + 5)
        def _():
            combine(0)

        return carry

    lax.fori_loop(0, PIECES + LAG4, step, 0)

    lc[...] = lowt[...].T.reshape(2, 512, 128)
    lcc = rcopy(lc.at[1 - c], lr, lcsend, lcrecv, sibling)
    lcc.start()
    combine(1)
    lcc.wait_recv()
    lo[y] = (lc[c] + lr[...]).astype(BF16)
    locopies = [rcopy(lo.at[y], lo.at[y], losend.at[k], lorecv.at[k], at_y(d)) for k, d in enumerate((yr, yl, yo))]
    lowaits = [rcopy(lo.at[d], lo.at[d], losend.at[k], lorecv.at[k], at_y(yr)) for k, d in enumerate((yl, yr, yo))]
    for cp in locopies:
        cp.start()
    for cp in lowaits:
        cp.wait_recv()
    low_ref[...] = lo[...]
    for k in range(1, 8):
        rarrive(k).wait_recv()
    back = (rbk[0].astype(F32) + rbk[1].astype(F32)).reshape(EXPERTS * PAD, 768) * slotw_s[...]
    high = back.astype(BF16)
    rest = (back - high.astype(F32)).astype(BF16)
    mixed_ref[...] = (dot_t(pick_s[...], high) + dot_t(pick_s[...], rest)).astype(BF16)

    for k in range(1, 8):
        zcopy(k).wait_send()
        zscopy(k).wait_send()
        rcopy_back(k).wait_send()
    for cp in wcopies + sycopies + locopies + [lcc]:
        cp.wait_send()
    for k in range(3):
        sxcopy(k).wait_send()
    for h in range(2):
        for r in (1, 2):
            xcopy(h, r).wait_send()
            xforward(h, r).wait_send()

    def drain(i, carry):
        for kind in range(10):
            ycopy(kind, i).wait_send()

        @pl.when(i % 4 > 0)
        def _():
            ccopy(i).wait_send()

        return carry

    lax.fori_loop(0, PIECES, drain, 0)


def moe(ids, route, tokens, cotangent, gate, up, down, projector):
    vm = lambda *shape: pltpu.VMEM(shape, BF16)
    vf = lambda *shape: pltpu.VMEM(shape, F32)
    sem = lambda *shape: pltpu.SemaphoreType.DMA(shape)
    n = PIECES
    scratch = [
        vm(4, 768, 256), vm(4, 768, 256), vm(2, 512, 768), vm(4, 768, 512),
        vm(192, 64), vf(192, 1), vm(4, PAD, 768), vm(4, 192, 128), vm(3, 192, 128), vm(4, PAD, 128),
        vm(2, 4, PAD, 768), vm(2, 4, PAD, 128), vm(n, 2, ROWS, 384), vm(4, 2, ROWS, 128),
        vm(n, 2, ROWS, 256), vm(n, 2, ROWS, 256), vm(n, 2, ROWS, 256), vf(n, 2, ROWS, 256), vf(n, 2, ROWS, 256),
        vm(n, ROWS, 256), vm(n, ROWS, 256), vm(n, 2, ROWS, 256), vm(n, 2, ROWS, 256),
        vm(n, 4, 2, ROWS, 128), vm(n, ROWS, 768), vm(n, ROWS, 768), vm(2, 4, PAD, 768), vm(2, 4, PAD, 768),
        vf(128, 1024), vf(2, 512, 128), vf(512, 128), vm(4, 512, 128),
        sem(6), sem(5), sem(5), sem(8), sem(8), sem(8), sem(8), sem(3), sem(3), sem(3), sem(3),
        sem(8), sem(8), sem(2, 2), sem(2, 2), sem(10, n), sem(10, n), sem(8), sem(8), sem(8), sem(8),
        pltpu.SemaphoreType.DMA, pltpu.SemaphoreType.DMA, sem(3), sem(3),
    ]
    vmem = pl.BlockSpec(memory_space=pltpu.VMEM)
    hbm = pl.BlockSpec(memory_space=pl.ANY)
    return pl.pallas_call(
        moe_kernel,
        out_shape=(
            jax.ShapeDtypeStruct((64, 768), BF16),
            jax.ShapeDtypeStruct((4, 512, 128), BF16),
        ),
        in_specs=[vmem, vmem, vmem, vmem, hbm, hbm, hbm, hbm],
        out_specs=(vmem, vmem),
        scratch_shapes=scratch,
        compiler_params=pltpu.CompilerParams(
            collective_id=0, has_side_effects=True, vmem_limit_bytes=52 * 1024 * 1024
        ),
        cost_estimate=pl.CostEstimate(flops=8_000_000_000, bytes_accessed=6_000_000, transcendentals=300_000),
        name="moe",
    )(ids, route, tokens, cotangent, gate, up, down, projector)


def update_kernel(expert_ref, low_ref, first_ref, second_ref, proj_ref, update_ref, new_first_ref, new_second_ref):
    low = jnp.concatenate([low_ref[d] for d in range(4)], axis=1).astype(F32)
    new_first = 0.9 * first_ref[...] + 0.1 * low
    new_second = 0.999 * second_ref[...] + 0.001 * low * low
    new_first_ref[...] = new_first
    new_second_ref[...] = new_second
    bias_one = 1.0 - 0.9**10
    bias_two = 1.0 - 0.999**10
    direction = new_first / bias_one / (jnp.sqrt(new_second / bias_two) + 1e-08)
    high = direction.astype(BF16)
    rest = (direction - high.astype(F32)).astype(BF16)
    basis = proj_ref[0]
    dims = (((1,), (1,)), ((), ()))
    update_ref[...] = lax.dot_general(high, basis, dims, preferred_element_type=F32) + lax.dot_general(
        rest, basis, dims, preferred_element_type=F32
    )


def update_step(expert, low, first, second, projector):
    rows = 128
    return pl.pallas_call(
        update_kernel,
        out_shape=(
            jax.ShapeDtypeStruct((512, 768), F32),
            jax.ShapeDtypeStruct((512, 512), F32),
            jax.ShapeDtypeStruct((512, 512), F32),
        ),
        grid_spec=pltpu.PrefetchScalarGridSpec(
            num_scalar_prefetch=1,
            grid=(512 // rows,),
            in_specs=[
                pl.BlockSpec((4, rows, 128), lambda i, e: (0, i, 0)),
                pl.BlockSpec((rows, 512), lambda i, e: (i, 0)),
                pl.BlockSpec((rows, 512), lambda i, e: (i, 0)),
                pl.BlockSpec((1, 768, 512), lambda i, e: (e[0], 0, 0)),
            ],
            out_specs=(
                pl.BlockSpec((rows, 768), lambda i, e: (i, 0)),
                pl.BlockSpec((rows, 512), lambda i, e: (i, 0)),
                pl.BlockSpec((rows, 512), lambda i, e: (i, 0)),
            ),
        ),
        cost_estimate=pl.CostEstimate(flops=800_000_000, bytes_accessed=7_000_000, transcendentals=300_000),
        name="update",
    )(expert, low, first, second, projector)


def body(
    tokens,
    cotangent,
    expert_ids,
    route_weights,
    gate_weight,
    up_weight,
    down_weight,
    projector,
    first_moment,
    second_moment,
):
    mixed, low = moe(
        expert_ids.T, route_weights.T, tokens, cotangent, gate_weight, up_weight, down_weight, projector
    )
    expert = (lax.axis_index("fsdp") // 16).astype(jnp.int32).reshape(1)
    update, new_first, new_second = update_step(expert, low, first_moment, second_moment, projector)
    return mixed, update, new_first, new_second


def solution(mesh):
    in_specs = (
        P("fsdp", "tp"),
        P("fsdp", "tp"),
        P("fsdp", None),
        P("fsdp", None),
        P("tp", "fsdp"),
        P("tp", "fsdp"),
        P("fsdp", "tp"),
        P(None, "tp", None),
        P("fsdp", None),
        P("fsdp", None),
    )
    out_specs = (P("fsdp", "tp"), P("fsdp", "tp"), P("fsdp", None), P("fsdp", None))
    return jax.shard_map(body, mesh=mesh, in_specs=in_specs, out_specs=out_specs, check_vma=False)
```

```python
import jax
import jax.numpy as jnp
from jax import lax
from jax.experimental import pallas as pl
from jax.experimental.pallas import tpu as pltpu
from jax.sharding import PartitionSpec as P

EXPERTS = 4
MOST = 36
MAIN, REST, BLOCK = 32, 16, 112
PAD = MAIN + REST
ROWS = 4 * MOST
PIECES = 8
RELZ = (0, 1, 2, 3, 4, -3, -2, -1)
LAG1, LAG2, LAG3, LAG4, LAG5 = 1, 2, 3, 4, 5
MESH = pl.DeviceIdType.MESH
F32, BF16 = jnp.float32, jnp.bfloat16


def dot(a, b):
    return jnp.dot(a, b, preferred_element_type=F32)


def dot_t(a, b):
    return lax.dot_general(a, b, (((0,), (0,)), ((), ())), preferred_element_type=F32)


def reach(v, size):
    return sum((v >= n * size).astype(jnp.int32) for n in range(1, 4))


def row_of(j, q):
    folded = jnp.where((j >= MAIN + 4 * q) & (j < MAIN + 4 * q + 4), j - 4 * q, -1)
    return jnp.where(j < MAIN, j, folded)


def matcher(shape, dense, q):
    d = lax.broadcasted_iota(jnp.int32, shape, dense)
    w = lax.broadcasted_iota(jnp.int32, shape, 1 - dense)
    ds, ws = reach(d, MOST), reach(w, PAD)
    return ((ds == ws) & (d - MOST * ds == row_of(w - PAD * ws, q))).astype(F32).astype(BF16)


def moe_kernel(
    ids_hbm, route_hbm, tok_hbm, cot_hbm, wg_hbm, wu_hbm, wd_hbm, proj_hbm,
    mixed_ref, low_ref,
    ids_ref, route_ref, tok_ref, cot_ref,
    wg, wu, wd, proj, pick_s, slotw_s, squeeze, widen, xs, xz, sps, spr, spz, sz,
    p2, pr, pll, qa, po, ra, rb, fl, fr, hd, ob, cb, eb, rbk, lowt, lc, lr, lo,
    lsem, wsend, wrecv, zsend, zrecv, zssend, zsrecv, sysend, syrecv, sxsend, sxrecv,
    xsend, xrecv, ysend, yrecv, csend, crecv, rsend, rrecv, lcsend, lcrecv, losend, lorecv,
):
    f = lax.axis_index("fsdp")
    y = lax.axis_index("tp")
    z, x, c = f // 8, (f // 2) % 4, f % 2
    yr, yl, yo = (y + 1) % 4, (y + 3) % 4, (y + 2) % 4

    def at_y(yy):
        return (f, yy)

    def at_x(step):
        return (z * 8 + ((x + step) % 4) * 2 + c, y)

    def at_z(zz):
        return (zz * 8 + x * 2 + c, y)

    def plane(k, sign):
        rel = jnp.where(k < 5, k, k - 8)
        return (z + 8 + sign * rel) % 8

    sibling = (z * 8 + x * 2 + (1 - c), y)

    def rcopy(src, dst, send, recv, dev):
        return pltpu.make_async_remote_copy(
            src_ref=src, dst_ref=dst, send_sem=send, recv_sem=recv, device_id=dev, device_id_type=MESH
        )

    inputs = [
        pltpu.make_async_copy(s, d, lsem.at[n])
        for n, (s, d) in enumerate(((ids_hbm, ids_ref), (route_hbm, route_ref), (tok_hbm, tok_ref), (cot_hbm, cot_ref)))
    ]
    weights = []
    for k in range(2):
        cols = pl.ds(k * 256, 256)
        weights.append(pltpu.make_async_copy(wg_hbm.at[:, cols], wg.at[2 * c + k], lsem.at[4 + k]))
        weights.append(pltpu.make_async_copy(wu_hbm.at[:, cols], wu.at[2 * c + k], lsem.at[6 + k]))
    down_copy = pltpu.make_async_copy(wd_hbm, wd.at[c], lsem.at[8])
    proj_copy = pltpu.make_async_copy(proj_hbm, proj, lsem.at[9])
    for cp in inputs + weights + [proj_copy, down_copy]:
        cp.start()

    barrier = pltpu.get_barrier_semaphore()
    partners = [at_y(yr), at_y(yl), at_y(yo), at_x(1), at_x(3), at_x(2), sibling]
    partners += [at_z((z + k) % 8) for k in range(1, 8)]
    for dev in partners:
        pl.semaphore_signal(barrier, inc=1, device_id=dev, device_id_type=MESH)

    place = lax.broadcasted_iota(jnp.int32, (EXPERTS * PAD, 64), 0)
    place_e = reach(place, PAD)
    place_j = place - PAD * place_e
    earlier = (
        lax.broadcasted_iota(jnp.int32, (64, 64), 0) < lax.broadcasted_iota(jnp.int32, (64, 64), 1)
    ).astype(F32)
    for cp in inputs:
        cp.wait()
    named0 = (ids_ref[0:1, :] == place_e).astype(F32)
    named1 = (ids_ref[1:2, :] == place_e).astype(F32)
    named = named0 + named1
    weight = named0 * route_ref[0:1, :] + named1 * route_ref[1:2, :]
    before = dot(named.astype(BF16), earlier.astype(BF16))
    tail = 0.0
    for q in range(3):
        pick = jnp.where(before == row_of(place_j, q).astype(F32), named, 0.0)
        slotw_s[q] = jnp.sum(pick * weight, axis=1, keepdims=True)
        pick_s[q] = pick.astype(BF16)
        rows = dot(pick.astype(BF16), tok_ref[:, q * 256:(q + 1) * 256])
        rows = rows.reshape(EXPERTS, PAD, 256)
        xs[:, q * MAIN:(q + 1) * MAIN, :] = rows[:, :MAIN].astype(BF16)
        tail = tail + rows[:, MAIN:]
    xs[:, 3 * MAIN:, :] = tail.astype(BF16)

    pl.semaphore_wait(barrier, len(partners))

    def zcopy(k):
        there = plane(k, -1)
        return rcopy(xs.at[there // 2], xz.at[k, 0], zsend.at[k], zrecv.at[k], at_z(there))

    def xcopy(k, r):
        return rcopy(xz.at[k, 0], xz.at[k, r], xsend.at[r, k], xrecv.at[r, k], at_x({2: 1, 1: 3, 3: 2}[r]))

    def spread(k):
        for r in (2, 1, 3):
            xcopy(k, r).start()

    xz[0, 0] = xs[z // 2]
    spread(0)
    for k in range(1, PIECES):
        zcopy(k).start()

    remote = []
    for k in range(2):
        cols = pl.ds(k * 256, 256)
        remote.append((wg_hbm.at[:, cols], wg, 2 * c + k, 2 * (1 - c) + k))
        remote.append((wu_hbm.at[:, cols], wu, 2 * c + k, 2 * (1 - c) + k))
    remote.append((wd_hbm, wd, c, 1 - c))
    wcopies = [rcopy(s, d.at[mine], wsend.at[n], wrecv.at[n], sibling) for n, (s, d, mine, _) in enumerate(remote)]
    wwaits = [rcopy(s, d.at[theirs], wsend.at[n], wrecv.at[n], sibling) for n, (s, d, _, theirs) in enumerate(remote)]
    for cp in wcopies:
        cp.start()

    for q in range(3):
        squeeze[q] = matcher((ROWS, 4 * PAD), 0, q)
        widen[q] = matcher((4 * PAD, ROWS), 1, q)
    lowt[...] = jnp.zeros_like(lowt)

    def zscopy(k):
        there = plane(k, -1)
        return rcopy(spz.at[there // 2], sz.at[0, k], zssend.at[k], zsrecv.at[k], at_z(there))

    sycopies = [
        rcopy(sps.at[d], spr.at[k], sysend.at[k], syrecv.at[k], at_y(d)) for k, d in enumerate((yr, yl, yo))
    ]

    def sxcopy(k):
        return rcopy(sz.at[0], sz.at[(2, 1, 3)[k]], sxsend.at[k], sxrecv.at[k], at_x((1, 3, 2)[k]))

    def project():
        proj_copy.wait()
        scaled = (dot(pick_s[0], cot_ref[...]) * slotw_s[0]).astype(BF16)
        for e in range(EXPERTS):
            part = dot(scaled[e * PAD:(e + 1) * PAD], proj[e]).astype(BF16)
            for d in range(4):
                sps[d, e * PAD:(e + 1) * PAD, :] = part[:, d * 128:(d + 1) * 128]
        for cp in sycopies:
            cp.start()

    def project_send():
        for cp in sycopies:
            cp.wait_recv()
        total = sps[y].astype(F32)
        for k in range(3):
            total = total + spr[k].astype(F32)
        spz[...] = total.astype(BF16).reshape(EXPERTS, PAD, 128)
        for k in range(1, PIECES):
            zscopy(k).start()
        sz[0, 0] = spz[z // 2]

    def project_spread():
        for k in range(1, PIECES):
            zscopy(k).wait_recv()
        for k in range(3):
            sxcopy(k).start()

    for cp in weights:
        cp.wait()
    for cp in wwaits[:4]:
        cp.wait_recv()

    def ycopy(kind, i):
        src, dst, dev = {
            0: lambda: (p2.at[i, 0], ra.at[i], yr),
            1: lambda: (p2.at[i, 1], rb.at[i], yl),
            2: lambda: (pr.at[i, 1], fl.at[i, 1], yr),
            3: lambda: (pll.at[i, 0], fr.at[i, 0], yl),
            4: lambda: (pr.at[i, 0], fl.at[i, 0], yr),
            5: lambda: (pll.at[i, 1], fr.at[i, 1], yl),
            6: lambda: (hd.at[i, y], hd.at[i, y], yr),
            7: lambda: (hd.at[i, y], hd.at[i, y], yl),
            8: lambda: (hd.at[i, yl, 0], hd.at[i, yl, 0], yr),
            9: lambda: (hd.at[i, yr, 1], hd.at[i, yr, 1], yl),
        }[kind]()
        return rcopy(src, dst, ysend.at[kind, i], yrecv.at[kind, i], at_y(dev))

    def yarrive(kind, i):
        if kind < 6:
            ycopy(kind, i).wait_recv()
            return
        dst = {
            6: lambda: hd.at[i, yl],
            7: lambda: hd.at[i, yr],
            8: lambda: hd.at[i, yo, 0],
            9: lambda: hd.at[i, yo, 1],
        }[kind]()
        rcopy(dst, dst, ysend.at[kind, i], yrecv.at[kind, i], at_y(yr)).wait_recv()

    def stage0(i):
        for r in range(1, 4):
            xcopy(i, r).wait_recv()
        chunks = []
        for q in range(3):
            parts = []
            for r in range(4):
                parts += [xz[i, r, q * MAIN:(q + 1) * MAIN, :], xz[i, r, 3 * MAIN:, :]]
            chunks.append(dot(squeeze[q], jnp.concatenate(parts, axis=0)).astype(BF16))
        v = jnp.concatenate(chunks, axis=1)
        p2[i, 0] = dot(v, wg[yo]).astype(BF16)
        ycopy(0, i).start()
        p2[i, 1] = dot(v, wu[yo]).astype(BF16)
        ycopy(1, i).start()
        pr[i, 1] = dot(v, wu[yr]).astype(BF16)
        ycopy(2, i).start()
        pll[i, 0] = dot(v, wg[yl]).astype(BF16)
        ycopy(3, i).start()
        qa[i, 0] = dot(v, wg[yr])
        qa[i, 1] = dot(v, wu[yl])
        po[i, 0] = dot(v, wg[y])
        po[i, 1] = dot(v, wu[y])

    def stage1(i):
        yarrive(0, i)
        pr[i, 0] = (qa[i, 0] + ra[i].astype(F32)).astype(BF16)
        ycopy(4, i).start()
        yarrive(1, i)
        pll[i, 1] = (qa[i, 1] + rb[i].astype(F32)).astype(BF16)
        ycopy(5, i).start()

    def stage2(i):
        for kind in (2, 3, 4, 5):
            yarrive(kind, i)
        g = po[i, 0] + fl[i, 0].astype(F32) + fr[i, 0].astype(F32)
        u = po[i, 1] + fl[i, 1].astype(F32) + fr[i, 1].astype(F32)
        hidden = (g / (1.0 + jnp.exp(-g)) * u).astype(BF16)
        hd[i, y, 0] = hidden[:, :128]
        hd[i, y, 1] = hidden[:, 128:]
        ycopy(6, i).start()
        ycopy(7, i).start()

    def stage3(i):
        yarrive(6, i)
        ycopy(8, i).start()
        yarrive(7, i)
        ycopy(9, i).start()

    def ccopy(i, r):
        slot = {1: 2, 2: 1, 3: 3}[r]
        return rcopy(ob.at[i, r], cb.at[i, slot], csend.at[slot, i], crecv.at[slot, i], at_x({1: 1, 2: 3, 3: 2}[r]))

    def stage4(i):
        yarrive(8, i)
        yarrive(9, i)
        hidden = jnp.concatenate([hd[i, d, k] for d in range(4) for k in range(2)], axis=1)
        part = dot(hidden, wd[...].reshape(1024, 768)).astype(BF16)
        tail = 0.0
        for q in range(3):
            wide = dot(widen[q], part[:, q * 256:(q + 1) * 256]).reshape(4, PAD, 256)
            ob[i, :, q * MAIN:(q + 1) * MAIN, :] = wide[:, :MAIN].astype(BF16)
            tail = tail + wide[:, MAIN:]
        ob[i, :, 3 * MAIN:, :] = tail.astype(BF16)
        for r in range(1, 4):
            ccopy(i, r).start()
        rows = dot(squeeze[0], jnp.concatenate([sz[r, i] for r in range(4)], axis=0)).astype(BF16)
        lowt[...] += dot_t(rows, hidden)

    def rcopy_back(k):
        return rcopy(eb.at[k], rbk.at[z % 2, z // 2], rsend.at[k], rrecv.at[k], at_z(plane(k, 1)))

    def rarrive(k):
        come = plane(k, -1)
        dst = rbk.at[come % 2, come // 2]
        return rcopy(dst, dst, rsend.at[k], rrecv.at[k], at_z((z + 1) % 8))

    def stage5(i):
        for r in range(1, 4):
            ccopy(i, r).wait_recv()
        total = ob[i, 0].astype(F32)
        for r in range(1, 4):
            total = total + cb[i, r].astype(F32)
        eb[i] = total.astype(BF16)

        @pl.when(i > 0)
        def _():
            rcopy_back(i).start()

        @pl.when(i == 0)
        def _():
            rbk[z % 2, z // 2] = eb[0]

    def step(it, carry):
        def run(stage, lag):
            @pl.when((it >= lag) & (it < lag + PIECES))
            def _():
                stage(it - lag)

        run(stage3, LAG3)
        run(stage2, LAG2)
        run(stage1, LAG1)
        run(stage0, 0)

        @pl.when(it + 1 < PIECES)
        def _():
            zcopy(it + 1).wait_recv()
            spread(it + 1)

        @pl.when(it == 0)
        def _():
            project()

        @pl.when(it == 1)
        def _():
            project_send()

        @pl.when(it == 3)
        def _():
            project_spread()

        @pl.when(it == LAG4)
        def _():
            for k in range(3):
                sxcopy(k).wait_recv()
            down_copy.wait()
            wwaits[4].wait_recv()

        run(stage4, LAG4)
        run(stage5, LAG5)
        return carry

    lax.fori_loop(0, PIECES + LAG4, step, 0)

    lc[...] = lowt[...].T.reshape(2, 512, 128)
    lcc = rcopy(lc.at[1 - c], lr, lcsend, lcrecv, sibling)
    lcc.start()
    for i in range(PIECES + LAG4 - LAG5, PIECES):
        stage5(i)
    lcc.wait_recv()
    lo[y] = (lc[c] + lr[...]).astype(BF16)
    locopies = [rcopy(lo.at[y], lo.at[y], losend.at[k], lorecv.at[k], at_y(d)) for k, d in enumerate((yr, yl, yo))]
    lowaits = [rcopy(lo.at[d], lo.at[d], losend.at[k], lorecv.at[k], at_y(yr)) for k, d in enumerate((yl, yr, yo))]
    for cp in locopies:
        cp.start()
    for cp in lowaits:
        cp.wait_recv()
    low_ref[...] = lo[...]
    for k in range(1, PIECES):
        rarrive(k).wait_recv()
    for q in range(3):
        parts = []
        for e in range(EXPERTS):
            for part in (slice(q * MAIN, (q + 1) * MAIN), slice(3 * MAIN, BLOCK)):
                parts.append(rbk[0, e, part, :].astype(F32) + rbk[1, e, part, :].astype(F32))
        back = jnp.concatenate(parts, axis=0) * slotw_s[q]
        high = back.astype(BF16)
        rest = (back - high.astype(F32)).astype(BF16)
        mixed_ref[:, q * 256:(q + 1) * 256] = (dot_t(pick_s[q], high) + dot_t(pick_s[q], rest)).astype(BF16)

    for cp in wcopies + sycopies + locopies + [lcc]:
        cp.wait_send()
    for k in range(3):
        sxcopy(k).wait_send()

    def drain(i, carry):
        for kind in range(10):
            ycopy(kind, i).wait_send()
        for r in range(1, 4):
            ccopy(i, r).wait_send()
            xcopy(i, r).wait_send()

        @pl.when(i > 0)
        def _():
            zcopy(i).wait_send()
            zscopy(i).wait_send()
            rcopy_back(i).wait_send()

        return carry

    lax.fori_loop(0, PIECES, drain, 0)


def moe(ids, route, tokens, cotangent, gate, up, down, projector):
    vm = lambda *shape: pltpu.VMEM(shape, BF16)
    vf = lambda *shape: pltpu.VMEM(shape, F32)
    sem = lambda *shape: pltpu.SemaphoreType.DMA(shape)
    n = PIECES
    scratch = [
        pltpu.VMEM((2, 64), jnp.int32), vf(2, 64), vm(64, 768), vm(64, 768),
        vm(4, 768, 256), vm(4, 768, 256), vm(2, 512, 768), vm(4, 768, 512),
        vm(3, 192, 64), vf(3, 192, 1), vm(3, ROWS, 192), vm(3, 192, ROWS),
        vm(4, BLOCK, 256), vm(n, 4, BLOCK, 256), vm(4, 192, 128), vm(3, 192, 128), vm(4, PAD, 128), vm(4, n, PAD, 128),
        vm(n, 2, ROWS, 256), vm(n, 2, ROWS, 256), vm(n, 2, ROWS, 256), vf(n, 2, ROWS, 256), vf(n, 2, ROWS, 256),
        vm(n, ROWS, 256), vm(n, ROWS, 256), vm(n, 2, ROWS, 256), vm(n, 2, ROWS, 256),
        vm(n, 4, 2, ROWS, 128), vm(n, 4, BLOCK, 256), vm(n, 4, BLOCK, 256), vm(n, BLOCK, 256), vm(2, 4, BLOCK, 256),
        vf(128, 1024), vf(2, 512, 128), vf(512, 128), vm(4, 512, 128),
        sem(10), sem(5), sem(5), sem(n), sem(n), sem(n), sem(n), sem(3), sem(3), sem(3), sem(3),
        sem(4, n), sem(4, n), sem(10, n), sem(10, n), sem(4, n), sem(4, n), sem(n), sem(n),
        pltpu.SemaphoreType.DMA, pltpu.SemaphoreType.DMA, sem(3), sem(3),
    ]
    vmem = pl.BlockSpec(memory_space=pltpu.VMEM)
    hbm = pl.BlockSpec(memory_space=pl.ANY)
    return pl.pallas_call(
        moe_kernel,
        out_shape=(
            jax.ShapeDtypeStruct((64, 768), BF16),
            jax.ShapeDtypeStruct((4, 512, 128), BF16),
        ),
        in_specs=[hbm] * 8,
        out_specs=(vmem, vmem),
        scratch_shapes=scratch,
        compiler_params=pltpu.CompilerParams(
            collective_id=0, has_side_effects=True, vmem_limit_bytes=52 * 1024 * 1024
        ),
        cost_estimate=pl.CostEstimate(flops=8_000_000_000, bytes_accessed=6_000_000, transcendentals=300_000),
        name="moe",
    )(ids, route, tokens, cotangent, gate, up, down, projector)


def update_kernel(expert_ref, low_ref, first_ref, second_ref, proj_ref, update_ref, new_first_ref, new_second_ref):
    low = jnp.concatenate([low_ref[d] for d in range(4)], axis=1).astype(F32)
    new_first = 0.9 * first_ref[...] + 0.1 * low
    new_second = 0.999 * second_ref[...] + 0.001 * low * low
    new_first_ref[...] = new_first
    new_second_ref[...] = new_second
    bias_one = 1.0 - 0.9**10
    bias_two = 1.0 - 0.999**10
    direction = new_first / bias_one / (jnp.sqrt(new_second / bias_two) + 1e-08)
    high = direction.astype(BF16)
    rest = (direction - high.astype(F32)).astype(BF16)
    basis = proj_ref[0]
    dims = (((1,), (1,)), ((), ()))
    update_ref[...] = lax.dot_general(high, basis, dims, preferred_element_type=F32) + lax.dot_general(
        rest, basis, dims, preferred_element_type=F32
    )


def update_step(expert, low, first, second, projector):
    rows = 128
    return pl.pallas_call(
        update_kernel,
        out_shape=(
            jax.ShapeDtypeStruct((512, 768), F32),
            jax.ShapeDtypeStruct((512, 512), F32),
            jax.ShapeDtypeStruct((512, 512), F32),
        ),
        grid_spec=pltpu.PrefetchScalarGridSpec(
            num_scalar_prefetch=1,
            grid=(512 // rows,),
            in_specs=[
                pl.BlockSpec((4, rows, 128), lambda i, e: (0, i, 0)),
                pl.BlockSpec((rows, 512), lambda i, e: (i, 0)),
                pl.BlockSpec((rows, 512), lambda i, e: (i, 0)),
                pl.BlockSpec((1, 768, 512), lambda i, e: (e[0], 0, 0)),
            ],
            out_specs=(
                pl.BlockSpec((rows, 768), lambda i, e: (i, 0)),
                pl.BlockSpec((rows, 512), lambda i, e: (i, 0)),
                pl.BlockSpec((rows, 512), lambda i, e: (i, 0)),
            ),
        ),
        cost_estimate=pl.CostEstimate(flops=800_000_000, bytes_accessed=7_000_000, transcendentals=300_000),
        name="update",
    )(expert, low, first, second, projector)


def body(
    tokens,
    cotangent,
    expert_ids,
    route_weights,
    gate_weight,
    up_weight,
    down_weight,
    projector,
    first_moment,
    second_moment,
):
    mixed, low = moe(
        expert_ids.T, route_weights.T, tokens, cotangent, gate_weight, up_weight, down_weight, projector
    )
    expert = (lax.axis_index("fsdp") // 16).astype(jnp.int32).reshape(1)
    update, new_first, new_second = update_step(expert, low, first_moment, second_moment, projector)
    return mixed, update, new_first, new_second


def solution(mesh):
    in_specs = (
        P("fsdp", "tp"),
        P("fsdp", "tp"),
        P("fsdp", None),
        P("fsdp", None),
        P("tp", "fsdp"),
        P("tp", "fsdp"),
        P("fsdp", "tp"),
        P(None, "tp", None),
        P("fsdp", None),
        P("fsdp", None),
    )
    out_specs = (P("fsdp", "tp"), P("fsdp", "tp"), P("fsdp", None), P("fsdp", None))
    return jax.shard_map(body, mesh=mesh, in_specs=in_specs, out_specs=out_specs, check_vma=False)
```

```python
import jax
import jax.numpy as jnp
from jax import lax
from jax.experimental import pallas as pl
from jax.experimental.pallas import tpu as pltpu
from jax.sharding import PartitionSpec as P

EXPERTS = 4
MOST = 36
MAIN, REST, BLOCK = 32, 16, 112
SLIM = 2 * MAIN + REST
PAD = MAIN + REST
ROWS = 4 * MOST
PIECES = 8
RELZ = (0, 1, 2, -2, 3, -3, 4, -1)
LAG1, LAG2, LAG3, LAG4, LAG5 = 1, 2, 3, 4, 5
MESH = pl.DeviceIdType.MESH
F32, BF16 = jnp.float32, jnp.bfloat16


def dot(a, b):
    return jnp.dot(a, b, preferred_element_type=F32)


def dot_t(a, b):
    return lax.dot_general(a, b, (((0,), (0,)), ((), ())), preferred_element_type=F32)


def reach(v, size):
    return sum((v >= n * size).astype(jnp.int32) for n in range(1, 4))


def row_of(j, q):
    folded = jnp.where((j >= MAIN + 4 * q) & (j < MAIN + 4 * q + 4), j - 4 * q, -1)
    return jnp.where(j < MAIN, j, folded)


def matcher(shape, dense, q):
    d = lax.broadcasted_iota(jnp.int32, shape, dense)
    w = lax.broadcasted_iota(jnp.int32, shape, 1 - dense)
    ds, ws = reach(d, MOST), reach(w, PAD)
    return ((ds == ws) & (d - MOST * ds == row_of(w - PAD * ws, q))).astype(F32).astype(BF16)


def moe_kernel(
    ids_hbm, route_hbm, tok_hbm, cot_hbm, wg_hbm, wu_hbm, wd_hbm, proj_hbm,
    mixed_ref, low_ref,
    ids_ref, route_ref, tok_ref, cot_ref,
    wg, wu, wd, proj, pick_s, slotw_s, squeeze, widen, xs, xz, sps, spr, spz, sz,
    p2, pr, pll, qa, po, ra, rb, fl, fr, hd, ob, cb, eb, rbk, lowa, lc, lr,
    lsem, wsend, wrecv, zsend, zrecv, zssend, zsrecv, sysend, syrecv, sgsend, sgrecv, sxsend, sxrecv,
    xsend, xrecv, ysend, yrecv, csend, crecv, rsend, rrecv, lcsend, lcrecv,
):
    f = lax.axis_index("fsdp")
    y = lax.axis_index("tp")
    z, x, c = f // 8, (f // 2) % 4, f % 2
    yr, yl, yo = (y + 1) % 4, (y + 3) % 4, (y + 2) % 4

    def at_y(yy):
        return (f, yy)

    def at_x(step):
        return (z * 8 + ((x + step) % 4) * 2 + c, y)

    def at_z(zz):
        return (zz * 8 + x * 2 + c, y)

    def plane(k, sign):
        if isinstance(k, int):
            return (z + 8 + sign * RELZ[k]) % 8
        rel = jnp.int32(RELZ[0])
        for n in range(1, PIECES):
            rel = jnp.where(k == n, RELZ[n], rel)
        return (z + 8 + sign * rel) % 8

    sibling = (z * 8 + x * 2 + (1 - c), y)

    def rcopy(src, dst, send, recv, dev):
        return pltpu.make_async_remote_copy(
            src_ref=src, dst_ref=dst, send_sem=send, recv_sem=recv, device_id=dev, device_id_type=MESH
        )

    inputs = [
        pltpu.make_async_copy(s, d, lsem.at[n])
        for n, (s, d) in enumerate(((ids_hbm, ids_ref), (route_hbm, route_ref), (tok_hbm, tok_ref), (cot_hbm, cot_ref)))
    ]
    weights = []
    for k in range(2):
        cols = pl.ds(k * 256, 256)
        weights.append(pltpu.make_async_copy(wg_hbm.at[:, cols], wg.at[2 * c + k], lsem.at[4 + k]))
        weights.append(pltpu.make_async_copy(wu_hbm.at[:, cols], wu.at[2 * c + k], lsem.at[6 + k]))
    down_copy = pltpu.make_async_copy(wd_hbm, wd.at[c], lsem.at[8])
    proj_copy = pltpu.make_async_copy(proj_hbm, proj, lsem.at[9])
    for cp in inputs + weights + [proj_copy, down_copy]:
        cp.start()

    barrier = pltpu.get_barrier_semaphore()
    partners = [at_z((z + k) % 8) for k in (4, 3, 5, 2, 6, 1, 7)]
    partners += [at_y(yo), at_x(2), at_y(yr), at_y(yl), at_x(1), at_x(3), sibling]
    for dev in partners:
        pl.semaphore_signal(barrier, inc=1, device_id=dev, device_id_type=MESH)

    place = lax.broadcasted_iota(jnp.int32, (EXPERTS * PAD, 64), 0)
    place_e = reach(place, PAD)
    place_j = place - PAD * place_e
    earlier = (
        lax.broadcasted_iota(jnp.int32, (64, 64), 0) < lax.broadcasted_iota(jnp.int32, (64, 64), 1)
    ).astype(F32)
    for cp in inputs:
        cp.wait()
    named0 = (ids_ref[0:1, :] == place_e).astype(F32)
    named1 = (ids_ref[1:2, :] == place_e).astype(F32)
    named = named0 + named1
    weight = named0 * route_ref[0:1, :] + named1 * route_ref[1:2, :]
    before = dot(named.astype(BF16), earlier.astype(BF16))
    tail = 0.0
    for q in range(3):
        pick = jnp.where(before == row_of(place_j, q).astype(F32), named, 0.0)
        slotw_s[q] = jnp.sum(pick * weight, axis=1, keepdims=True)
        pick_s[q] = pick.astype(BF16)
        rows = dot(pick.astype(BF16), tok_ref[:, q * 256:(q + 1) * 256])
        rows = rows.reshape(EXPERTS, PAD, 256)
        xs[:, q * MAIN:(q + 1) * MAIN, :] = rows[:, :MAIN].astype(BF16)
        tail = tail + rows[:, MAIN:]
    xs[:, 3 * MAIN:, :] = tail.astype(BF16)

    for q in range(3):
        squeeze[q] = matcher((ROWS, 4 * PAD), 0, q)
        widen[q] = matcher((4 * PAD, ROWS), 1, q)
    lowa[...] = jnp.zeros_like(lowa)

    pl.semaphore_wait(barrier, len(partners))

    def zcopy(k):
        there = plane(k, -1)
        return rcopy(xs.at[there // 2], xz.at[k, 0], zsend.at[k], zrecv.at[k], at_z(there))

    def xcopy(k, r):
        return rcopy(xz.at[k, 0], xz.at[k, r], xsend.at[r, k], xrecv.at[r, k], at_x({2: 1, 1: 3, 3: 2}[r]))

    def spread(k):
        for r in (2, 1, 3):
            xcopy(k, r).start()

    xz[0, 0] = xs[z // 2]
    spread(0)
    for k in range(1, PIECES):
        zcopy(k).start()

    remote = []
    for k in range(2):
        cols = pl.ds(k * 256, 256)
        remote.append((wg_hbm.at[:, cols], wg, 2 * c + k, 2 * (1 - c) + k))
        remote.append((wu_hbm.at[:, cols], wu, 2 * c + k, 2 * (1 - c) + k))
    remote.append((wd_hbm, wd, c, 1 - c))
    wcopies = [rcopy(s, d.at[mine], wsend.at[n], wrecv.at[n], sibling) for n, (s, d, mine, _) in enumerate(remote)]
    wwaits = [rcopy(s, d.at[theirs], wsend.at[n], wrecv.at[n], sibling) for n, (s, d, _, theirs) in enumerate(remote)]
    for cp in wcopies:
        cp.start()

    def zscopy(k):
        there = plane(k, -1)
        return rcopy(spz.at[there // 2], sz.at[0, k], zssend.at[k], zsrecv.at[k], at_z(there))

    sycopies = [
        rcopy(sps.at[d], spr.at[k], sysend.at[k], syrecv.at[k], at_y(d)) for k, d in enumerate((yr, yl, yo))
    ]
    sgcopies = [
        rcopy(spz.at[y], spz.at[y], sgsend.at[k], sgrecv.at[k], at_y(d)) for k, d in enumerate((yr, yl, yo))
    ]
    sgwaits = [
        rcopy(spz.at[d], spz.at[d], sgsend.at[k], sgrecv.at[k], at_y(yr)) for k, d in enumerate((yl, yr, yo))
    ]

    def sxcopy(k, r):
        return rcopy(sz.at[0, k], sz.at[r, k], sxsend.at[r, k], sxrecv.at[r, k], at_x({2: 1, 1: 3, 3: 2}[r]))

    def project():
        proj_copy.wait()
        tails = [0.0] * EXPERTS
        for q in range(2):
            scaled = (dot(pick_s[q], cot_ref[...]) * slotw_s[q]).astype(BF16)
            for e in range(EXPERTS):
                part = dot(scaled[e * PAD:(e + 1) * PAD], proj[e, :, q * 256:(q + 1) * 256])
                sps[e, q * MAIN:(q + 1) * MAIN, :] = part[:MAIN].astype(BF16)
                tails[e] = tails[e] + part[MAIN:]
        for e in range(EXPERTS):
            sps[e, 2 * MAIN:, :] = tails[e].astype(BF16)
        for cp in sycopies:
            cp.start()

    def project_sum():
        for cp in sycopies:
            cp.wait_recv()
        total = sps[y].astype(F32)
        for k in range(3):
            total = total + spr[k].astype(F32)
        spz[y] = total.astype(BF16)
        for cp in sgcopies:
            cp.start()

    def project_send():
        for cp in sgwaits:
            cp.wait_recv()
        for k in range(1, PIECES):
            zscopy(k).start()
        sz[0, 0] = spz[z // 2]

    project()
    for cp in weights:
        cp.wait()
    for cp in wwaits[:4]:
        cp.wait_recv()

    def ycopy(kind, i):
        src, dst, dev = {
            0: lambda: (p2.at[i, 0], ra.at[i], yr),
            1: lambda: (p2.at[i, 1], rb.at[i], yl),
            2: lambda: (pr.at[i, 1], fl.at[i, 1], yr),
            3: lambda: (pll.at[i, 0], fr.at[i, 0], yl),
            4: lambda: (pr.at[i, 0], fl.at[i, 0], yr),
            5: lambda: (pll.at[i, 1], fr.at[i, 1], yl),
            6: lambda: (hd.at[i, y], hd.at[i, y], yr),
            7: lambda: (hd.at[i, y], hd.at[i, y], yl),
            8: lambda: (hd.at[i, yl, 0], hd.at[i, yl, 0], yr),
            9: lambda: (hd.at[i, yr, 1], hd.at[i, yr, 1], yl),
        }[kind]()
        return rcopy(src, dst, ysend.at[kind, i], yrecv.at[kind, i], at_y(dev))

    def yarrive(kind, i):
        if kind < 6:
            ycopy(kind, i).wait_recv()
            return
        dst = {
            6: lambda: hd.at[i, yl],
            7: lambda: hd.at[i, yr],
            8: lambda: hd.at[i, yo, 0],
            9: lambda: hd.at[i, yo, 1],
        }[kind]()
        rcopy(dst, dst, ysend.at[kind, i], yrecv.at[kind, i], at_y(yr)).wait_recv()

    def stage0(i):
        for r in range(1, 4):
            xcopy(i, r).wait_recv()
        chunks = []
        for q in range(3):
            parts = []
            for r in range(4):
                parts += [xz[i, r, q * MAIN:(q + 1) * MAIN, :], xz[i, r, 3 * MAIN:, :]]
            chunks.append(dot(squeeze[q], jnp.concatenate(parts, axis=0)).astype(BF16))
        v = jnp.concatenate(chunks, axis=1)
        p2[i, 0] = dot(v, wg[yo]).astype(BF16)
        ycopy(0, i).start()
        p2[i, 1] = dot(v, wu[yo]).astype(BF16)
        ycopy(1, i).start()
        pr[i, 1] = dot(v, wu[yr]).astype(BF16)
        ycopy(2, i).start()
        pll[i, 0] = dot(v, wg[yl]).astype(BF16)
        ycopy(3, i).start()
        qa[i, 0] = dot(v, wg[yr])
        qa[i, 1] = dot(v, wu[yl])
        po[i, 0] = dot(v, wg[y])
        po[i, 1] = dot(v, wu[y])

    def stage1(i):
        yarrive(0, i)
        pr[i, 0] = (qa[i, 0] + ra[i].astype(F32)).astype(BF16)
        ycopy(4, i).start()
        yarrive(1, i)
        pll[i, 1] = (qa[i, 1] + rb[i].astype(F32)).astype(BF16)
        ycopy(5, i).start()

    def stage2(i):
        for kind in (2, 3, 4, 5):
            yarrive(kind, i)
        g = po[i, 0] + fl[i, 0].astype(F32) + fr[i, 0].astype(F32)
        u = po[i, 1] + fl[i, 1].astype(F32) + fr[i, 1].astype(F32)
        hidden = (g / (1.0 + jnp.exp(-g)) * u).astype(BF16)
        hd[i, y, 0] = hidden[:, :128]
        hd[i, y, 1] = hidden[:, 128:]
        ycopy(6, i).start()
        ycopy(7, i).start()

    def stage3(i):
        yarrive(6, i)
        ycopy(8, i).start()
        yarrive(7, i)
        ycopy(9, i).start()

    def ccopy(i, r):
        slot = {1: 2, 2: 1, 3: 3}[r]
        return rcopy(ob.at[i, r], cb.at[i, slot], csend.at[slot, i], crecv.at[slot, i], at_x({1: 1, 2: 3, 3: 2}[r]))

    lcc = rcopy(lc, lr, lcsend, lcrecv, sibling)

    def stage4(i):
        yarrive(8, i)
        yarrive(9, i)
        hidden = jnp.concatenate([hd[i, d, k] for d in range(4) for k in range(2)], axis=1)
        for r in range(1, 4):
            sxcopy(i, r).wait_recv()
        chunks = []
        for q in range(2):
            parts = []
            for r in range(4):
                parts += [sz[r, i, q * MAIN:(q + 1) * MAIN, :], sz[r, i, 2 * MAIN:, :]]
            chunks.append(dot(squeeze[q], jnp.concatenate(parts, axis=0)).astype(BF16))
        rows = jnp.concatenate(chunks, axis=1)
        for k in range(2):
            lowa[k] += dot_t(hidden[:, k * 512:(k + 1) * 512], rows)

        @pl.when(i == PIECES - 1)
        def _():
            lc[...] = lowa[1 - c].astype(BF16)
            lcc.start()

        part = dot(hidden, wd[...].reshape(1024, 768)).astype(BF16)
        tail = 0.0
        for q in range(3):
            wide = dot(widen[q], part[:, q * 256:(q + 1) * 256]).reshape(4, PAD, 256)
            ob[i, :, q * MAIN:(q + 1) * MAIN, :] = wide[:, :MAIN].astype(BF16)
            tail = tail + wide[:, MAIN:]
        ob[i, :, 3 * MAIN:, :] = tail.astype(BF16)
        for r in range(1, 4):
            ccopy(i, r).start()

    def rcopy_back(k):
        return rcopy(eb.at[k], rbk.at[z % 2, z // 2], rsend.at[k], rrecv.at[k], at_z(plane(k, 1)))

    def rarrive(k):
        come = plane(k, -1)
        dst = rbk.at[come % 2, come // 2]
        return rcopy(dst, dst, rsend.at[k], rrecv.at[k], at_z((z + 1) % 8))

    def stage5(i):
        for r in range(1, 4):
            ccopy(i, r).wait_recv()
        total = ob[i, 0].astype(F32)
        for r in range(1, 4):
            total = total + cb[i, r].astype(F32)
        eb[i] = total.astype(BF16)

        @pl.when(i > 0)
        def _():
            rcopy_back(i).start()

        @pl.when(i == 0)
        def _():
            rbk[z % 2, z // 2] = eb[0]

    def step(it, carry):
        def run(stage, lag):
            @pl.when((it >= lag) & (it < lag + PIECES))
            def _():
                stage(it - lag)

        run(stage3, LAG3)
        run(stage2, LAG2)
        run(stage1, LAG1)
        run(stage0, 0)

        @pl.when(it + 1 < PIECES)
        def _():
            zcopy(it + 1).wait_recv()
            spread(it + 1)

        @pl.when(it == 0)
        def _():
            project_sum()

        @pl.when(it == 1)
        def _():
            project_send()

        @pl.when((it >= 2) & (it < 2 + PIECES))
        def _():
            @pl.when(it > 2)
            def _():
                zscopy(it - 2).wait_recv()

            for r in (2, 1, 3):
                sxcopy(it - 2, r).start()

        @pl.when(it == LAG4)
        def _():
            down_copy.wait()
            wwaits[4].wait_recv()

        run(stage4, LAG4)
        run(stage5, LAG5)
        return carry

    lax.fori_loop(0, PIECES + LAG4, step, 0)

    for i in range(PIECES + LAG4 - LAG5, PIECES):
        stage5(i)
    lcc.wait_recv()
    low_ref[...] = (lowa[c] + lr[...].astype(F32)).astype(BF16)
    for k in range(1, PIECES):
        rarrive(k).wait_recv()
    for q in range(3):
        parts = []
        for e in range(EXPERTS):
            for part in (slice(q * MAIN, (q + 1) * MAIN), slice(3 * MAIN, BLOCK)):
                parts.append(rbk[0, e, part, :].astype(F32) + rbk[1, e, part, :].astype(F32))
        back = jnp.concatenate(parts, axis=0) * slotw_s[q]
        high = back.astype(BF16)
        rest = (back - high.astype(F32)).astype(BF16)
        mixed_ref[:, q * 256:(q + 1) * 256] = (dot_t(pick_s[q], high) + dot_t(pick_s[q], rest)).astype(BF16)

    for cp in wcopies + sycopies + sgcopies + [lcc]:
        cp.wait_send()

    def drain(i, carry):
        for kind in range(10):
            ycopy(kind, i).wait_send()
        for r in range(1, 4):
            ccopy(i, r).wait_send()
            xcopy(i, r).wait_send()
            sxcopy(i, r).wait_send()

        @pl.when(i > 0)
        def _():
            zcopy(i).wait_send()
            zscopy(i).wait_send()
            rcopy_back(i).wait_send()

        return carry

    lax.fori_loop(0, PIECES, drain, 0)


def moe(ids, route, tokens, cotangent, gate, up, down, projector):
    vm = lambda *shape: pltpu.VMEM(shape, BF16)
    vf = lambda *shape: pltpu.VMEM(shape, F32)
    sem = lambda *shape: pltpu.SemaphoreType.DMA(shape)
    n = PIECES
    scratch = [
        pltpu.VMEM((2, 64), jnp.int32), vf(2, 64), vm(64, 768), vm(64, 768),
        vm(4, 768, 256), vm(4, 768, 256), vm(2, 512, 768), vm(4, 768, 512),
        vm(3, 192, 64), vf(3, 192, 1), vm(3, ROWS, 192), vm(3, 192, ROWS),
        vm(4, BLOCK, 256), vm(n, 4, BLOCK, 256), vm(4, SLIM, 256), vm(3, SLIM, 256), vm(4, SLIM, 256), vm(4, n, SLIM, 256),
        vm(n, 2, ROWS, 256), vm(n, 2, ROWS, 256), vm(n, 2, ROWS, 256), vf(n, 2, ROWS, 256), vf(n, 2, ROWS, 256),
        vm(n, ROWS, 256), vm(n, ROWS, 256), vm(n, 2, ROWS, 256), vm(n, 2, ROWS, 256),
        vm(n, 4, 2, ROWS, 128), vm(n, 4, BLOCK, 256), vm(n, 4, BLOCK, 256), vm(n, BLOCK, 256), vm(2, 4, BLOCK, 256),
        vf(2, 512, 512), vm(512, 512), vm(512, 512),
        sem(10), sem(5), sem(5), sem(n), sem(n), sem(n), sem(n), sem(3), sem(3), sem(3), sem(3), sem(4, n), sem(4, n),
        sem(4, n), sem(4, n), sem(10, n), sem(10, n), sem(4, n), sem(4, n), sem(n), sem(n),
        pltpu.SemaphoreType.DMA, pltpu.SemaphoreType.DMA,
    ]
    vmem = pl.BlockSpec(memory_space=pltpu.VMEM)
    hbm = pl.BlockSpec(memory_space=pl.ANY)
    return pl.pallas_call(
        moe_kernel,
        out_shape=(
            jax.ShapeDtypeStruct((64, 768), BF16),
            jax.ShapeDtypeStruct((512, 512), BF16),
        ),
        in_specs=[hbm] * 8,
        out_specs=(vmem, vmem),
        scratch_shapes=scratch,
        compiler_params=pltpu.CompilerParams(
            collective_id=0, has_side_effects=True, vmem_limit_bytes=65000 * 1024
        ),
        cost_estimate=pl.CostEstimate(flops=8_000_000_000, bytes_accessed=6_000_000, transcendentals=300_000),
        name="moe",
    )(ids, route, tokens, cotangent, gate, up, down, projector)


def update_kernel(
    expert_ref, low_ref, first_ref, second_ref, proj_ref, mixed_ref, update_ref, new_first_ref, new_second_ref, out_ref
):
    out_ref[...] = mixed_ref[...]
    low = low_ref[...].astype(F32)
    new_first = 0.9 * first_ref[...] + 0.1 * low
    new_second = 0.999 * second_ref[...] + 0.001 * low * low
    new_first_ref[...] = new_first
    new_second_ref[...] = new_second
    bias_one = 1.0 - 0.9**10
    bias_two = 1.0 - 0.999**10
    direction = new_first / bias_one / (jnp.sqrt(new_second / bias_two) + 1e-08)
    high = direction.astype(BF16)
    rest = (direction - high.astype(F32)).astype(BF16)
    basis = proj_ref[0]
    dims = (((1,), (1,)), ((), ()))
    update_ref[...] = lax.dot_general(high, basis, dims, preferred_element_type=F32) + lax.dot_general(
        rest, basis, dims, preferred_element_type=F32
    )


def update_step(expert, low, first, second, projector, mixed):
    rows = 256
    return pl.pallas_call(
        update_kernel,
        out_shape=(
            jax.ShapeDtypeStruct((512, 768), F32),
            jax.ShapeDtypeStruct((512, 512), F32),
            jax.ShapeDtypeStruct((512, 512), F32),
            jax.ShapeDtypeStruct((64, 768), BF16),
        ),
        grid_spec=pltpu.PrefetchScalarGridSpec(
            num_scalar_prefetch=1,
            grid=(512 // rows,),
            in_specs=[
                pl.BlockSpec((rows, 512), lambda i, e: (i, 0)),
                pl.BlockSpec((rows, 512), lambda i, e: (i, 0)),
                pl.BlockSpec((rows, 512), lambda i, e: (i, 0)),
                pl.BlockSpec((1, 768, 512), lambda i, e: (e[0], 0, 0)),
                pl.BlockSpec((rows // 8, 768), lambda i, e: (i, 0)),
            ],
            out_specs=(
                pl.BlockSpec((rows, 768), lambda i, e: (i, 0)),
                pl.BlockSpec((rows, 512), lambda i, e: (i, 0)),
                pl.BlockSpec((rows, 512), lambda i, e: (i, 0)),
                pl.BlockSpec((rows // 8, 768), lambda i, e: (i, 0)),
            ),
        ),
        cost_estimate=pl.CostEstimate(flops=800_000_000, bytes_accessed=7_000_000, transcendentals=300_000),
        name="update",
    )(expert, low, first, second, projector, mixed)


def body(
    tokens,
    cotangent,
    expert_ids,
    route_weights,
    gate_weight,
    up_weight,
    down_weight,
    projector,
    first_moment,
    second_moment,
):
    mixed, low = moe(
        expert_ids.T, route_weights.T, tokens, cotangent, gate_weight, up_weight, down_weight, projector
    )
    expert = (lax.axis_index("fsdp") // 16).astype(jnp.int32).reshape(1)
    update, new_first, new_second, mixed = update_step(
        expert, low, first_moment, second_moment, projector, mixed
    )
    return mixed, update, new_first, new_second


def solution(mesh):
    in_specs = (
        P("fsdp", "tp"),
        P("fsdp", "tp"),
        P("fsdp", None),
        P("fsdp", None),
        P("tp", "fsdp"),
        P("tp", "fsdp"),
        P("fsdp", "tp"),
        P(None, "tp", None),
        P("fsdp", None),
        P("fsdp", None),
    )
    out_specs = (P("fsdp", "tp"), P("fsdp", "tp"), P("fsdp", None), P("fsdp", None))
    return jax.shard_map(body, mesh=mesh, in_specs=in_specs, out_specs=out_specs, check_vma=False)
```

```python
import jax
import jax.numpy as jnp
from jax import lax
from jax.experimental import pallas as pl
from jax.experimental.pallas import tpu as pltpu
from jax.sharding import PartitionSpec as P

EXPERTS = 4
MOST = 36
MAIN, REST, BLOCK = 32, 16, 112
SLIM = 2 * MAIN + REST
PAD = MAIN + REST
ROWS = 4 * MOST
PIECES = 8
RELZ = (0, 1, 2, -2, 3, -3, 4, -1)
LAG1, LAG2, LAG3, LAG4, LAG5 = 1, 2, 3, 4, 5
MESH = pl.DeviceIdType.MESH
F32, BF16 = jnp.float32, jnp.bfloat16


def dot(a, b):
    return jnp.dot(a, b, preferred_element_type=F32)


def dot_t(a, b):
    return lax.dot_general(a, b, (((0,), (0,)), ((), ())), preferred_element_type=F32)


def reach(v, size):
    return sum((v >= n * size).astype(jnp.int32) for n in range(1, 4))


def row_of(j, q):
    folded = jnp.where((j >= MAIN + 4 * q) & (j < MAIN + 4 * q + 4), j - 4 * q, -1)
    return jnp.where(j < MAIN, j, folded)


def matcher(shape, dense, q):
    d = lax.broadcasted_iota(jnp.int32, shape, dense)
    w = lax.broadcasted_iota(jnp.int32, shape, 1 - dense)
    ds, ws = reach(d, MOST), reach(w, PAD)
    return ((ds == ws) & (d - MOST * ds == row_of(w - PAD * ws, q))).astype(F32).astype(BF16)


def moe_kernel(
    ids_hbm, route_hbm, tok_hbm, cot_hbm, wg_hbm, wu_hbm, wd_hbm, proj_hbm,
    mixed_ref, low_ref,
    ids_ref, route_ref, tok_ref, cot_ref,
    wg, wu, wd, proj, pick_s, slotw_s, squeeze, widen, xs, xz, sps, spr, spz, sz,
    p2, pr, pll, qa, po, ra, rb, fl, fr, hd, ob, cb, eb, rbk, lowa, lc, lr,
    lsem, wsend, wrecv, zsend, zrecv, zssend, zsrecv, sysend, syrecv, sgsend, sgrecv, sxsend, sxrecv,
    xsend, xrecv, ysend, yrecv, csend, crecv, rsend, rrecv, lcsend, lcrecv,
):
    f = lax.axis_index("fsdp")
    y = lax.axis_index("tp")
    z, x, c = f // 8, (f // 2) % 4, f % 2
    yr, yl, yo = (y + 1) % 4, (y + 3) % 4, (y + 2) % 4

    def at_y(yy):
        return (f, yy)

    def at_x(step):
        return (z * 8 + ((x + step) % 4) * 2 + c, y)

    def at_z(zz):
        return (zz * 8 + x * 2 + c, y)

    def plane(k, sign):
        if isinstance(k, int):
            return (z + 8 + sign * RELZ[k]) % 8
        rel = jnp.int32(RELZ[0])
        for n in range(1, PIECES):
            rel = jnp.where(k == n, RELZ[n], rel)
        return (z + 8 + sign * rel) % 8

    sibling = (z * 8 + x * 2 + (1 - c), y)

    def rcopy(src, dst, send, recv, dev):
        return pltpu.make_async_remote_copy(
            src_ref=src, dst_ref=dst, send_sem=send, recv_sem=recv, device_id=dev, device_id_type=MESH
        )

    inputs = [
        pltpu.make_async_copy(s, d, lsem.at[n])
        for n, (s, d) in enumerate(((ids_hbm, ids_ref), (route_hbm, route_ref), (tok_hbm, tok_ref), (cot_hbm, cot_ref)))
    ]
    weights = []
    for k in range(2):
        cols = pl.ds(k * 256, 256)
        weights.append(pltpu.make_async_copy(wg_hbm.at[:, cols], wg.at[2 * c + k], lsem.at[4 + k]))
        weights.append(pltpu.make_async_copy(wu_hbm.at[:, cols], wu.at[2 * c + k], lsem.at[6 + k]))
    down_copy = pltpu.make_async_copy(wd_hbm, wd.at[c], lsem.at[8])
    proj_copy = pltpu.make_async_copy(proj_hbm, proj, lsem.at[9])
    for cp in inputs + weights + [proj_copy, down_copy]:
        cp.start()

    barrier = pltpu.get_barrier_semaphore()
    partners = [at_z((z + k) % 8) for k in (4, 3, 5, 2, 6, 1, 7)]
    partners += [at_y(yo), at_x(2), at_y(yr), at_y(yl), at_x(1), at_x(3), sibling]
    for dev in partners:
        pl.semaphore_signal(barrier, inc=1, device_id=dev, device_id_type=MESH)

    place = lax.broadcasted_iota(jnp.int32, (EXPERTS * PAD, 64), 0)
    place_e = reach(place, PAD)
    place_j = place - PAD * place_e
    earlier = (
        lax.broadcasted_iota(jnp.int32, (64, 64), 0) < lax.broadcasted_iota(jnp.int32, (64, 64), 1)
    ).astype(F32)
    for cp in inputs:
        cp.wait()
    named0 = (ids_ref[0:1, :] == place_e).astype(F32)
    named1 = (ids_ref[1:2, :] == place_e).astype(F32)
    named = named0 + named1
    weight = named0 * route_ref[0:1, :] + named1 * route_ref[1:2, :]
    before = dot(named.astype(BF16), earlier.astype(BF16))
    tail = 0.0
    for q in range(3):
        pick = jnp.where(before == row_of(place_j, q).astype(F32), named, 0.0)
        slotw_s[q] = jnp.sum(pick * weight, axis=1, keepdims=True)
        pick_s[q] = pick.astype(BF16)
        rows = dot(pick.astype(BF16), tok_ref[:, q * 256:(q + 1) * 256])
        rows = rows.reshape(EXPERTS, PAD, 256)
        xs[:, q * MAIN:(q + 1) * MAIN, :] = rows[:, :MAIN].astype(BF16)
        tail = tail + rows[:, MAIN:]
    xs[:, 3 * MAIN:, :] = tail.astype(BF16)

    for q in range(3):
        squeeze[q] = matcher((ROWS, 4 * PAD), 0, q)
        widen[q] = matcher((4 * PAD, ROWS), 1, q)
    lowa[...] = jnp.zeros_like(lowa)

    proj_copy.wait()
    tails = [0.0] * EXPERTS
    for q in range(2):
        scaled = (dot(pick_s[q], cot_ref[...]) * slotw_s[q]).astype(BF16)
        for e in range(EXPERTS):
            part = dot(scaled[e * PAD:(e + 1) * PAD], proj[e, :, q * 256:(q + 1) * 256])
            sps[e, q * MAIN:(q + 1) * MAIN, :] = part[:MAIN].astype(BF16)
            tails[e] = tails[e] + part[MAIN:]
    for e in range(EXPERTS):
        sps[e, 2 * MAIN:, :] = tails[e].astype(BF16)

    pl.semaphore_wait(barrier, len(partners))

    def zcopy(k):
        there = plane(k, -1)
        return rcopy(xs.at[there // 2], xz.at[k, 0], zsend.at[k], zrecv.at[k], at_z(there))

    def xcopy(k, r):
        return rcopy(xz.at[k, 0], xz.at[k, r], xsend.at[r, k], xrecv.at[r, k], at_x({2: 1, 1: 3, 3: 2}[r]))

    def spread(k):
        for r in (2, 1, 3):
            xcopy(k, r).start()

    xz[0, 0] = xs[z // 2]
    spread(0)

    remote = []
    for k in range(2):
        cols = pl.ds(k * 256, 256)
        remote.append((wg_hbm.at[:, cols], wg, 2 * c + k, 2 * (1 - c) + k))
        remote.append((wu_hbm.at[:, cols], wu, 2 * c + k, 2 * (1 - c) + k))
    remote.append((wd_hbm, wd, c, 1 - c))
    wcopies = [rcopy(s, d.at[mine], wsend.at[n], wrecv.at[n], sibling) for n, (s, d, mine, _) in enumerate(remote)]
    wwaits = [rcopy(s, d.at[theirs], wsend.at[n], wrecv.at[n], sibling) for n, (s, d, _, theirs) in enumerate(remote)]
    for cp in wcopies:
        cp.start()
    for k in range(1, PIECES):
        zcopy(k).start()

    def zscopy(k):
        there = plane(k, -1)
        return rcopy(spz.at[there // 2], sz.at[0, k], zssend.at[k], zsrecv.at[k], at_z(there))

    sycopies = [
        rcopy(sps.at[d], spr.at[k], sysend.at[k], syrecv.at[k], at_y(d)) for k, d in enumerate((yr, yl, yo))
    ]
    sgcopies = [
        rcopy(spz.at[y], spz.at[y], sgsend.at[k], sgrecv.at[k], at_y(d)) for k, d in enumerate((yr, yl, yo))
    ]
    sgwaits = [
        rcopy(spz.at[d], spz.at[d], sgsend.at[k], sgrecv.at[k], at_y(yr)) for k, d in enumerate((yl, yr, yo))
    ]

    for cp in sycopies:
        cp.start()

    def sxcopy(k, r):
        return rcopy(sz.at[0, k], sz.at[r, k], sxsend.at[r, k], sxrecv.at[r, k], at_x({2: 1, 1: 3, 3: 2}[r]))

    def project_sum():
        for cp in sycopies:
            cp.wait_recv()
        total = sps[y].astype(F32)
        for k in range(3):
            total = total + spr[k].astype(F32)
        spz[y] = total.astype(BF16)
        for cp in sgcopies:
            cp.start()

    def project_send():
        for cp in sgwaits:
            cp.wait_recv()
        for k in range(1, PIECES):
            zscopy(k).start()
        sz[0, 0] = spz[z // 2]

    project_sum()
    for cp in weights:
        cp.wait()
    for cp in wwaits[:4]:
        cp.wait_recv()

    def ycopy(kind, i):
        src, dst, dev = {
            0: lambda: (p2.at[i, 0], ra.at[i], yr),
            1: lambda: (p2.at[i, 1], rb.at[i], yl),
            2: lambda: (pr.at[i, 1], fl.at[i, 1], yr),
            3: lambda: (pll.at[i, 0], fr.at[i, 0], yl),
            4: lambda: (pr.at[i, 0], fl.at[i, 0], yr),
            5: lambda: (pll.at[i, 1], fr.at[i, 1], yl),
            6: lambda: (hd.at[i, y], hd.at[i, y], yr),
            7: lambda: (hd.at[i, y], hd.at[i, y], yl),
            8: lambda: (hd.at[i, yl, 0], hd.at[i, yl, 0], yr),
            9: lambda: (hd.at[i, yr, 1], hd.at[i, yr, 1], yl),
        }[kind]()
        return rcopy(src, dst, ysend.at[kind, i], yrecv.at[kind, i], at_y(dev))

    def yarrive(kind, i):
        if kind < 6:
            ycopy(kind, i).wait_recv()
            return
        dst = {
            6: lambda: hd.at[i, yl],
            7: lambda: hd.at[i, yr],
            8: lambda: hd.at[i, yo, 0],
            9: lambda: hd.at[i, yo, 1],
        }[kind]()
        rcopy(dst, dst, ysend.at[kind, i], yrecv.at[kind, i], at_y(yr)).wait_recv()

    def stage0(i):
        for r in range(1, 4):
            xcopy(i, r).wait_recv()
        chunks = []
        for q in range(3):
            parts = []
            for r in range(4):
                parts += [xz[i, r, q * MAIN:(q + 1) * MAIN, :], xz[i, r, 3 * MAIN:, :]]
            chunks.append(dot(squeeze[q], jnp.concatenate(parts, axis=0)).astype(BF16))
        v = jnp.concatenate(chunks, axis=1)
        p2[i, 0] = dot(v, wg[yo]).astype(BF16)
        ycopy(0, i).start()
        p2[i, 1] = dot(v, wu[yo]).astype(BF16)
        ycopy(1, i).start()
        pr[i, 1] = dot(v, wu[yr]).astype(BF16)
        pll[i, 0] = dot(v, wg[yl]).astype(BF16)
        qa[i, 0] = dot(v, wg[yr])
        qa[i, 1] = dot(v, wu[yl])
        po[i, 0] = dot(v, wg[y])
        po[i, 1] = dot(v, wu[y])
        ycopy(3, i).start()
        ycopy(2, i).start()

    def stage1(i):
        yarrive(0, i)
        pr[i, 0] = (qa[i, 0] + ra[i].astype(F32)).astype(BF16)
        ycopy(4, i).start()
        yarrive(1, i)
        pll[i, 1] = (qa[i, 1] + rb[i].astype(F32)).astype(BF16)
        ycopy(5, i).start()

    def stage2(i):
        for kind in (2, 3, 4, 5):
            yarrive(kind, i)
        g = po[i, 0] + fl[i, 0].astype(F32) + fr[i, 0].astype(F32)
        u = po[i, 1] + fl[i, 1].astype(F32) + fr[i, 1].astype(F32)
        hidden = (g / (1.0 + jnp.exp(-g)) * u).astype(BF16)
        hd[i, y, 0] = hidden[:, :128]
        hd[i, y, 1] = hidden[:, 128:]
        ycopy(6, i).start()
        ycopy(7, i).start()

    def stage3(i):
        yarrive(6, i)
        ycopy(8, i).start()
        yarrive(7, i)
        ycopy(9, i).start()

    def ccopy(i, r):
        slot = {1: 2, 2: 1, 3: 3}[r]
        return rcopy(ob.at[i, r], cb.at[i, slot], csend.at[slot, i], crecv.at[slot, i], at_x({1: 1, 2: 3, 3: 2}[r]))

    lcc = rcopy(lc, lr, lcsend, lcrecv, sibling)

    def stage4(i):
        yarrive(8, i)
        yarrive(9, i)
        hidden = jnp.concatenate([hd[i, d, k] for d in range(4) for k in range(2)], axis=1)
        part = dot(hidden, wd[...].reshape(1024, 768)).astype(BF16)
        tail = 0.0
        for q in range(3):
            wide = dot(widen[q], part[:, q * 256:(q + 1) * 256]).reshape(4, PAD, 256)
            ob[i, :, q * MAIN:(q + 1) * MAIN, :] = wide[:, :MAIN].astype(BF16)
            tail = tail + wide[:, MAIN:]
        ob[i, :, 3 * MAIN:, :] = tail.astype(BF16)
        for r in range(1, 4):
            ccopy(i, r).start()

        for r in range(1, 4):
            sxcopy(i, r).wait_recv()
        chunks = []
        for q in range(2):
            parts = []
            for r in range(4):
                parts += [sz[r, i, q * MAIN:(q + 1) * MAIN, :], sz[r, i, 2 * MAIN:, :]]
            chunks.append(dot(squeeze[q], jnp.concatenate(parts, axis=0)).astype(BF16))
        rows = jnp.concatenate(chunks, axis=1)
        for k in range(2):
            lowa[k] += dot_t(hidden[:, k * 512:(k + 1) * 512], rows)

        @pl.when(i == PIECES - 1)
        def _():
            lc[...] = lowa[1 - c].astype(BF16)
            lcc.start()

    def rcopy_back(k):
        return rcopy(eb.at[k], rbk.at[z % 2, z // 2], rsend.at[k], rrecv.at[k], at_z(plane(k, 1)))

    def rarrive(k):
        come = plane(k, -1)
        dst = rbk.at[come % 2, come // 2]
        return rcopy(dst, dst, rsend.at[k], rrecv.at[k], at_z((z + 1) % 8))

    def returned(i):
        for r in range(1, 4):
            ccopy(i, r).wait_send()

        @pl.when(i > 0)
        def _():
            rcopy_back(i).wait_send()

    def stage5(i):
        for kind in range(10):
            ycopy(kind, i).wait_send()
        for r in range(1, 4):
            xcopy(i, r).wait_send()
            sxcopy(i, r).wait_send()

        @pl.when(i > 0)
        def _():
            zcopy(i).wait_send()
            zscopy(i).wait_send()
            returned(i - 1)

        for r in range(1, 4):
            ccopy(i, r).wait_recv()
        total = ob[i, 0].astype(F32)
        for r in range(1, 4):
            total = total + cb[i, r].astype(F32)
        eb[i] = total.astype(BF16)

        @pl.when(i > 0)
        def _():
            rcopy_back(i).start()

        @pl.when(i == 0)
        def _():
            rbk[z % 2, z // 2] = eb[0]

    def step(it, carry):
        def run(stage, lag):
            @pl.when((it >= lag) & (it < lag + PIECES))
            def _():
                stage(it - lag)

        run(stage3, LAG3)
        run(stage2, LAG2)
        run(stage1, LAG1)
        run(stage0, 0)

        @pl.when(it + 1 < PIECES)
        def _():
            zcopy(it + 1).wait_recv()
            spread(it + 1)

        @pl.when(it == 0)
        def _():
            project_send()

        @pl.when((it >= 2) & (it < 2 + PIECES))
        def _():
            @pl.when(it > 2)
            def _():
                zscopy(it - 2).wait_recv()

            for r in (2, 1, 3):
                sxcopy(it - 2, r).start()

        @pl.when(it == LAG4)
        def _():
            down_copy.wait()
            wwaits[4].wait_recv()
            for cp in wcopies + sycopies + sgcopies:
                cp.wait_send()

        run(stage4, LAG4)
        run(stage5, LAG5)
        return carry

    lax.fori_loop(0, PIECES + LAG4, step, 0)

    for i in range(PIECES + LAG4 - LAG5, PIECES):
        stage5(i)
    lcc.wait_recv()
    low_ref[...] = (lowa[c] + lr[...].astype(F32)).astype(BF16)
    for k in range(1, PIECES):
        rarrive(k).wait_recv()
    for q in range(3):
        parts = []
        for e in range(EXPERTS):
            for part in (slice(q * MAIN, (q + 1) * MAIN), slice(3 * MAIN, BLOCK)):
                parts.append(rbk[0, e, part, :].astype(F32) + rbk[1, e, part, :].astype(F32))
        back = jnp.concatenate(parts, axis=0) * slotw_s[q]
        high = back.astype(BF16)
        rest = (back - high.astype(F32)).astype(BF16)
        mixed_ref[:, q * 256:(q + 1) * 256] = (dot_t(pick_s[q], high) + dot_t(pick_s[q], rest)).astype(BF16)

    lcc.wait_send()
    returned(PIECES - 1)


def moe(ids, route, tokens, cotangent, gate, up, down, projector):
    vm = lambda *shape: pltpu.VMEM(shape, BF16)
    vf = lambda *shape: pltpu.VMEM(shape, F32)
    sem = lambda *shape: pltpu.SemaphoreType.DMA(shape)
    n = PIECES
    scratch = [
        pltpu.VMEM((2, 64), jnp.int32), vf(2, 64), vm(64, 768), vm(64, 768),
        vm(4, 768, 256), vm(4, 768, 256), vm(2, 512, 768), vm(4, 768, 512),
        vm(3, 192, 64), vf(3, 192, 1), vm(3, ROWS, 192), vm(3, 192, ROWS),
        vm(4, BLOCK, 256), vm(n, 4, BLOCK, 256), vm(4, SLIM, 256), vm(3, SLIM, 256), vm(4, SLIM, 256), vm(4, n, SLIM, 256),
        vm(n, 2, ROWS, 256), vm(n, 2, ROWS, 256), vm(n, 2, ROWS, 256), vf(n, 2, ROWS, 256), vf(n, 2, ROWS, 256),
        vm(n, ROWS, 256), vm(n, ROWS, 256), vm(n, 2, ROWS, 256), vm(n, 2, ROWS, 256),
        vm(n, 4, 2, ROWS, 128), vm(n, 4, BLOCK, 256), vm(n, 4, BLOCK, 256), vm(n, BLOCK, 256), vm(2, 4, BLOCK, 256),
        vf(2, 512, 512), vm(512, 512), vm(512, 512),
        sem(10), sem(5), sem(5), sem(n), sem(n), sem(n), sem(n), sem(3), sem(3), sem(3), sem(3), sem(4, n), sem(4, n),
        sem(4, n), sem(4, n), sem(10, n), sem(10, n), sem(4, n), sem(4, n), sem(n), sem(n),
        pltpu.SemaphoreType.DMA, pltpu.SemaphoreType.DMA,
    ]
    vmem = pl.BlockSpec(memory_space=pltpu.VMEM)
    hbm = pl.BlockSpec(memory_space=pl.ANY)
    return pl.pallas_call(
        moe_kernel,
        out_shape=(
            jax.ShapeDtypeStruct((64, 768), BF16),
            jax.ShapeDtypeStruct((512, 512), BF16),
        ),
        in_specs=[hbm] * 8,
        out_specs=(vmem, vmem),
        scratch_shapes=scratch,
        compiler_params=pltpu.CompilerParams(
            collective_id=0, has_side_effects=True, vmem_limit_bytes=65000 * 1024
        ),
        cost_estimate=pl.CostEstimate(flops=8_000_000_000, bytes_accessed=6_000_000, transcendentals=300_000),
        name="moe",
    )(ids, route, tokens, cotangent, gate, up, down, projector)


def update_kernel(
    expert_ref, low_ref, first_ref, second_ref, proj_ref, mixed_ref, update_ref, new_first_ref, new_second_ref, out_ref
):
    out_ref[...] = mixed_ref[...]
    low = low_ref[...].astype(F32)
    new_first = 0.9 * first_ref[...] + 0.1 * low
    new_second = 0.999 * second_ref[...] + 0.001 * low * low
    new_first_ref[...] = new_first
    new_second_ref[...] = new_second
    bias_one = 1.0 - 0.9**10
    bias_two = 1.0 - 0.999**10
    direction = new_first / bias_one / (jnp.sqrt(new_second / bias_two) + 1e-08)
    high = direction.astype(BF16)
    rest = (direction - high.astype(F32)).astype(BF16)
    basis = proj_ref[0]
    dims = (((1,), (1,)), ((), ()))
    update_ref[...] = lax.dot_general(high, basis, dims, preferred_element_type=F32) + lax.dot_general(
        rest, basis, dims, preferred_element_type=F32
    )


def update_step(expert, low, first, second, projector, mixed):
    rows = 256
    return pl.pallas_call(
        update_kernel,
        out_shape=(
            jax.ShapeDtypeStruct((512, 768), F32),
            jax.ShapeDtypeStruct((512, 512), F32),
            jax.ShapeDtypeStruct((512, 512), F32),
            jax.ShapeDtypeStruct((64, 768), BF16),
        ),
        grid_spec=pltpu.PrefetchScalarGridSpec(
            num_scalar_prefetch=1,
            grid=(512 // rows,),
            in_specs=[
                pl.BlockSpec((rows, 512), lambda i, e: (i, 0)),
                pl.BlockSpec((rows, 512), lambda i, e: (i, 0)),
                pl.BlockSpec((rows, 512), lambda i, e: (i, 0)),
                pl.BlockSpec((1, 768, 512), lambda i, e: (e[0], 0, 0)),
                pl.BlockSpec((rows // 8, 768), lambda i, e: (i, 0)),
            ],
            out_specs=(
                pl.BlockSpec((rows, 768), lambda i, e: (i, 0)),
                pl.BlockSpec((rows, 512), lambda i, e: (i, 0)),
                pl.BlockSpec((rows, 512), lambda i, e: (i, 0)),
                pl.BlockSpec((rows // 8, 768), lambda i, e: (i, 0)),
            ),
        ),
        cost_estimate=pl.CostEstimate(flops=800_000_000, bytes_accessed=7_000_000, transcendentals=300_000),
        name="update",
    )(expert, low, first, second, projector, mixed)


def body(
    tokens,
    cotangent,
    expert_ids,
    route_weights,
    gate_weight,
    up_weight,
    down_weight,
    projector,
    first_moment,
    second_moment,
):
    mixed, low = moe(
        expert_ids.T, route_weights.T, tokens, cotangent, gate_weight, up_weight, down_weight, projector
    )
    expert = (lax.axis_index("fsdp") // 16).astype(jnp.int32).reshape(1)
    update, new_first, new_second, mixed = update_step(
        expert, low, first_moment, second_moment, projector, mixed
    )
    return mixed, update, new_first, new_second


def solution(mesh):
    in_specs = (
        P("fsdp", "tp"),
        P("fsdp", "tp"),
        P("fsdp", None),
        P("fsdp", None),
        P("tp", "fsdp"),
        P("tp", "fsdp"),
        P("fsdp", "tp"),
        P(None, "tp", None),
        P("fsdp", None),
        P("fsdp", None),
    )
    out_specs = (P("fsdp", "tp"), P("fsdp", "tp"), P("fsdp", None), P("fsdp", None))
    return jax.shard_map(body, mesh=mesh, in_specs=in_specs, out_specs=out_specs, check_vma=False)
```

```python
import jax
import jax.numpy as jnp
from jax import lax
from jax.experimental import pallas as pl
from jax.experimental.pallas import tpu as pltpu
from jax.sharding import PartitionSpec as P

EXPERTS = 4
MOST = 36
MAIN, REST, BLOCK = 32, 16, 112
SLIM = 2 * MAIN + REST
PAD = MAIN + REST
ROWS = 4 * MOST
PIECES = 8
RELZ = (0, 1, 2, -2, 3, -3, 4, -1)
LAG1, LAG2, LAG3, LAG4, LAG5 = 1, 2, 3, 4, 5
MESH = pl.DeviceIdType.MESH
F32, BF16 = jnp.float32, jnp.bfloat16


def dot(a, b):
    return jnp.dot(a, b, preferred_element_type=F32)


def dot_t(a, b):
    return lax.dot_general(a, b, (((0,), (0,)), ((), ())), preferred_element_type=F32)


def reach(v, size):
    return sum((v >= n * size).astype(jnp.int32) for n in range(1, 4))


def row_of(j, q):
    folded = jnp.where((j >= MAIN + 4 * q) & (j < MAIN + 4 * q + 4), j - 4 * q, -1)
    return jnp.where(j < MAIN, j, folded)


def matcher(shape, dense, q):
    d = lax.broadcasted_iota(jnp.int32, shape, dense)
    w = lax.broadcasted_iota(jnp.int32, shape, 1 - dense)
    ds, ws = reach(d, MOST), reach(w, PAD)
    return ((ds == ws) & (d - MOST * ds == row_of(w - PAD * ws, q))).astype(F32).astype(BF16)


def moe_kernel(
    ids_hbm, route_hbm, tok_hbm, cot_hbm, wg_hbm, wu_hbm, wd_hbm, proj_hbm,
    mixed_ref, low_ref,
    ids_ref, route_ref, tok_ref, cot_ref,
    wg, wu, wd, proj, pick_s, slotw_s, squeeze, widen, xs, xz, sps, spr, spz, sz,
    p2, pr, pll, qa, po, ra, rb, fl, fr, hd, ob, cb, eb, rbk, lowa, lc, lr,
    lsem, wsend, wrecv, zsend, zrecv, zssend, zsrecv, sysend, syrecv, sgsend, sgrecv, sxsend, sxrecv,
    xsend, xrecv, ysend, yrecv, csend, crecv, rsend, rrecv, lcsend, lcrecv,
):
    f = lax.axis_index("fsdp")
    y = lax.axis_index("tp")
    z, x, c = f // 8, (f // 2) % 4, f % 2
    yr, yl, yo = (y + 1) % 4, (y + 3) % 4, (y + 2) % 4

    def at_y(yy):
        return (f, yy)

    def at_x(step):
        return (z * 8 + ((x + step) % 4) * 2 + c, y)

    def at_z(zz):
        return (zz * 8 + x * 2 + c, y)

    def plane(k, sign):
        if isinstance(k, int):
            return (z + 8 + sign * RELZ[k]) % 8
        rel = jnp.int32(RELZ[0])
        for n in range(1, PIECES):
            rel = jnp.where(k == n, RELZ[n], rel)
        return (z + 8 + sign * rel) % 8

    sibling = (z * 8 + x * 2 + (1 - c), y)

    def rcopy(src, dst, send, recv, dev):
        return pltpu.make_async_remote_copy(
            src_ref=src, dst_ref=dst, send_sem=send, recv_sem=recv, device_id=dev, device_id_type=MESH
        )

    inputs = [
        pltpu.make_async_copy(s, d, lsem.at[n])
        for n, (s, d) in enumerate(((ids_hbm, ids_ref), (route_hbm, route_ref), (tok_hbm, tok_ref), (cot_hbm, cot_ref)))
    ]
    weights = []
    for k in range(2):
        cols = pl.ds(k * 256, 256)
        weights.append(pltpu.make_async_copy(wg_hbm.at[:, cols], wg.at[2 * c + k], lsem.at[4 + k]))
        weights.append(pltpu.make_async_copy(wu_hbm.at[:, cols], wu.at[2 * c + k], lsem.at[6 + k]))
    down_copy = pltpu.make_async_copy(wd_hbm, wd.at[c], lsem.at[8])
    proj_copy = pltpu.make_async_copy(proj_hbm, proj, lsem.at[9])
    for cp in inputs + weights + [proj_copy, down_copy]:
        cp.start()

    barrier = pltpu.get_barrier_semaphore()
    partners = [at_z((z + k) % 8) for k in (4, 3, 5, 2, 6, 1, 7)]
    partners += [at_y(yo), at_x(2), at_y(yr), at_y(yl), at_x(1), at_x(3), sibling]
    for dev in partners:
        pl.semaphore_signal(barrier, inc=1, device_id=dev, device_id_type=MESH)

    place = lax.broadcasted_iota(jnp.int32, (EXPERTS * PAD, 64), 0)
    place_e = reach(place, PAD)
    place_j = place - PAD * place_e
    earlier = (
        lax.broadcasted_iota(jnp.int32, (64, 64), 0) < lax.broadcasted_iota(jnp.int32, (64, 64), 1)
    ).astype(F32)
    for cp in inputs:
        cp.wait()
    named0 = (ids_ref[0:1, :] == place_e).astype(F32)
    named1 = (ids_ref[1:2, :] == place_e).astype(F32)
    named = named0 + named1
    weight = named0 * route_ref[0:1, :] + named1 * route_ref[1:2, :]
    before = dot(named.astype(BF16), earlier.astype(BF16))
    tail = 0.0
    for q in range(3):
        pick = jnp.where(before == row_of(place_j, q).astype(F32), named, 0.0)
        slotw_s[q] = jnp.sum(pick * weight, axis=1, keepdims=True)
        pick_s[q] = pick.astype(BF16)
        rows = dot(pick.astype(BF16), tok_ref[:, q * 256:(q + 1) * 256])
        rows = rows.reshape(EXPERTS, PAD, 256)
        xs[:, q * MAIN:(q + 1) * MAIN, :] = rows[:, :MAIN].astype(BF16)
        tail = tail + rows[:, MAIN:]
    xs[:, 3 * MAIN:, :] = tail.astype(BF16)

    for q in range(3):
        squeeze[q] = matcher((ROWS, 4 * PAD), 0, q)
        widen[q] = matcher((4 * PAD, ROWS), 1, q)
    lowa[...] = jnp.zeros_like(lowa)

    proj_copy.wait()
    tails = [0.0] * EXPERTS
    for q in range(2):
        scaled = (dot(pick_s[q], cot_ref[...]) * slotw_s[q]).astype(BF16)
        for e in range(EXPERTS):
            part = dot(scaled[e * PAD:(e + 1) * PAD], proj[e, :, q * 256:(q + 1) * 256])
            sps[e, q * MAIN:(q + 1) * MAIN, :] = part[:MAIN].astype(BF16)
            tails[e] = tails[e] + part[MAIN:]
    for e in range(EXPERTS):
        sps[e, 2 * MAIN:, :] = tails[e].astype(BF16)

    pl.semaphore_wait(barrier, len(partners))

    def zcopy(k):
        there = plane(k, -1)
        return rcopy(xs.at[there // 2], xz.at[k, 0], zsend.at[k], zrecv.at[k], at_z(there))

    def xcopy(k, r):
        return rcopy(xz.at[k, 0], xz.at[k, r], xsend.at[r, k], xrecv.at[r, k], at_x({2: 1, 1: 3, 3: 2}[r]))

    def spread(k):
        for r in (2, 1, 3):
            xcopy(k, r).start()

    xz[0, 0] = xs[z // 2]
    spread(0)

    remote = []
    for k in range(2):
        cols = pl.ds(k * 256, 256)
        remote.append((wg_hbm.at[:, cols], wg, 2 * c + k, 2 * (1 - c) + k))
        remote.append((wu_hbm.at[:, cols], wu, 2 * c + k, 2 * (1 - c) + k))
    remote.append((wd_hbm, wd, c, 1 - c))
    wcopies = [rcopy(s, d.at[mine], wsend.at[n], wrecv.at[n], sibling) for n, (s, d, mine, _) in enumerate(remote)]
    wwaits = [rcopy(s, d.at[theirs], wsend.at[n], wrecv.at[n], sibling) for n, (s, d, _, theirs) in enumerate(remote)]
    for cp in wcopies:
        cp.start()
    for k in range(1, PIECES):
        zcopy(k).start()

    def zscopy(k):
        there = plane(k, -1)
        return rcopy(spz.at[there // 2], sz.at[0, k], zssend.at[k], zsrecv.at[k], at_z(there))

    sycopies = [
        rcopy(sps.at[d], spr.at[k], sysend.at[k], syrecv.at[k], at_y(d)) for k, d in enumerate((yr, yl, yo))
    ]
    sgcopies = [
        rcopy(spz.at[y], spz.at[y], sgsend.at[k], sgrecv.at[k], at_y(d)) for k, d in enumerate((yr, yl, yo))
    ]
    sgwaits = [
        rcopy(spz.at[d], spz.at[d], sgsend.at[k], sgrecv.at[k], at_y(yr)) for k, d in enumerate((yl, yr, yo))
    ]

    for cp in sycopies:
        cp.start()

    def sxcopy(k, r):
        return rcopy(sz.at[0, k], sz.at[r, k], sxsend.at[r, k], sxrecv.at[r, k], at_x({2: 1, 1: 3, 3: 2}[r]))

    def project_sum():
        for cp in sycopies:
            cp.wait_recv()
        total = sps[y].astype(F32)
        for k in range(3):
            total = total + spr[k].astype(F32)
        spz[y] = total.astype(BF16)
        for cp in sgcopies:
            cp.start()

    def project_send():
        for cp in sgwaits:
            cp.wait_recv()
        for k in range(1, PIECES):
            zscopy(k).start()
        sz[0, 0] = spz[z // 2]

    project_sum()
    for cp in weights:
        cp.wait()
    for cp in wwaits[:4]:
        cp.wait_recv()

    def ycopy(kind, i):
        src, dst, dev = {
            0: lambda: (p2.at[i, 0], ra.at[i], yr),
            1: lambda: (p2.at[i, 1], rb.at[i], yl),
            2: lambda: (pr.at[i, 1], fl.at[i, 1], yr),
            3: lambda: (pll.at[i, 0], fr.at[i, 0], yl),
            4: lambda: (pr.at[i, 0], fl.at[i, 0], yr),
            5: lambda: (pll.at[i, 1], fr.at[i, 1], yl),
            6: lambda: (hd.at[i, y], hd.at[i, y], yr),
            7: lambda: (hd.at[i, y], hd.at[i, y], yl),
            8: lambda: (hd.at[i, yl, 0], hd.at[i, yl, 0], yr),
            9: lambda: (hd.at[i, yr, 1], hd.at[i, yr, 1], yl),
        }[kind]()
        return rcopy(src, dst, ysend.at[kind, i], yrecv.at[kind, i], at_y(dev))

    def yarrive(kind, i):
        if kind < 6:
            ycopy(kind, i).wait_recv()
            return
        dst = {
            6: lambda: hd.at[i, yl],
            7: lambda: hd.at[i, yr],
            8: lambda: hd.at[i, yo, 0],
            9: lambda: hd.at[i, yo, 1],
        }[kind]()
        rcopy(dst, dst, ysend.at[kind, i], yrecv.at[kind, i], at_y(yr)).wait_recv()

    def stage0(i):
        for r in range(1, 4):
            xcopy(i, r).wait_recv()
        chunks = []
        for q in range(3):
            parts = []
            for r in range(4):
                parts += [xz[i, r, q * MAIN:(q + 1) * MAIN, :], xz[i, r, 3 * MAIN:, :]]
            chunks.append(dot(squeeze[q], jnp.concatenate(parts, axis=0)).astype(BF16))
        v = jnp.concatenate(chunks, axis=1)
        p2[i, 0] = dot(v, wg[yo]).astype(BF16)
        ycopy(0, i).start()
        p2[i, 1] = dot(v, wu[yo]).astype(BF16)
        ycopy(1, i).start()
        pr[i, 1] = dot(v, wu[yr]).astype(BF16)
        pll[i, 0] = dot(v, wg[yl]).astype(BF16)
        qa[i, 0] = dot(v, wg[yr])
        qa[i, 1] = dot(v, wu[yl])
        po[i, 0] = dot(v, wg[y])
        po[i, 1] = dot(v, wu[y])
        ycopy(3, i).start()
        ycopy(2, i).start()

    def stage1(i):
        yarrive(0, i)
        pr[i, 0] = (qa[i, 0] + ra[i].astype(F32)).astype(BF16)
        ycopy(4, i).start()
        yarrive(1, i)
        pll[i, 1] = (qa[i, 1] + rb[i].astype(F32)).astype(BF16)
        ycopy(5, i).start()

    def stage2(i):
        for kind in (2, 3, 4, 5):
            yarrive(kind, i)
        g = po[i, 0] + fl[i, 0].astype(F32) + fr[i, 0].astype(F32)
        u = po[i, 1] + fl[i, 1].astype(F32) + fr[i, 1].astype(F32)
        hidden = (g / (1.0 + jnp.exp(-g)) * u).astype(BF16)
        hd[i, y, 0] = hidden[:, :128]
        hd[i, y, 1] = hidden[:, 128:]
        ycopy(6, i).start()
        ycopy(7, i).start()

    def stage3(i):
        yarrive(6, i)
        ycopy(8, i).start()
        yarrive(7, i)
        ycopy(9, i).start()

    def ccopy(i, r):
        slot = {1: 2, 2: 1, 3: 3}[r]
        return rcopy(ob.at[i, r], cb.at[i, slot], csend.at[slot, i], crecv.at[slot, i], at_x({1: 1, 2: 3, 3: 2}[r]))

    lcc = rcopy(lc, lr, lcsend, lcrecv, sibling)

    def stage4(i):
        yarrive(8, i)
        yarrive(9, i)
        hidden = jnp.concatenate([hd[i, d, k] for d in range(4) for k in range(2)], axis=1)
        part = dot(hidden, wd[...].reshape(1024, 768)).astype(BF16)
        tail = 0.0
        for q in range(3):
            wide = dot(widen[q], part[:, q * 256:(q + 1) * 256]).reshape(4, PAD, 256)
            ob[i, :, q * MAIN:(q + 1) * MAIN, :] = wide[:, :MAIN].astype(BF16)
            tail = tail + wide[:, MAIN:]
        ob[i, :, 3 * MAIN:, :] = tail.astype(BF16)
        for r in range(1, 4):
            ccopy(i, r).start()

        for r in range(1, 4):
            sxcopy(i, r).wait_recv()
        chunks = []
        for q in range(2):
            parts = []
            for r in range(4):
                parts += [sz[r, i, q * MAIN:(q + 1) * MAIN, :], sz[r, i, 2 * MAIN:, :]]
            chunks.append(dot(squeeze[q], jnp.concatenate(parts, axis=0)).astype(BF16))
        rows = jnp.concatenate(chunks, axis=1)
        for k in range(2):
            lowa[k] += dot_t(hidden[:, k * 512:(k + 1) * 512], rows)

        @pl.when(i == PIECES - 1)
        def _():
            lc[...] = lowa[1 - c].astype(BF16)
            lcc.start()

    def rcopy_back(k):
        return rcopy(eb.at[k], rbk.at[z % 2, z // 2], rsend.at[k], rrecv.at[k], at_z(plane(k, 1)))

    def rarrive(k):
        come = plane(k, -1)
        dst = rbk.at[come % 2, come // 2]
        return rcopy(dst, dst, rsend.at[k], rrecv.at[k], at_z((z + 1) % 8))

    def returned(i):
        for r in range(1, 4):
            ccopy(i, r).wait_send()

        @pl.when(i > 0)
        def _():
            rcopy_back(i).wait_send()

    def stage5(i):
        for kind in range(10):
            ycopy(kind, i).wait_send()
        for r in range(1, 4):
            xcopy(i, r).wait_send()
            sxcopy(i, r).wait_send()

        @pl.when(i > 0)
        def _():
            zcopy(i).wait_send()
            zscopy(i).wait_send()
            returned(i - 1)

        for r in range(1, 4):
            ccopy(i, r).wait_recv()
        total = ob[i, 0].astype(F32)
        for r in range(1, 4):
            total = total + cb[i, r].astype(F32)
        eb[i] = total.astype(BF16)

        @pl.when(i > 0)
        def _():
            rcopy_back(i).start()

        @pl.when(i == 0)
        def _():
            rbk[z % 2, z // 2] = eb[0]

    def step(it, carry):
        def run(stage, lag):
            @pl.when((it >= lag) & (it < lag + PIECES))
            def _():
                stage(it - lag)

        run(stage3, LAG3)
        run(stage2, LAG2)
        run(stage1, LAG1)
        @pl.when(it == LAG4)
        def _():
            down_copy.wait()
            wwaits[4].wait_recv()
            for cp in wcopies + sycopies + sgcopies:
                cp.wait_send()

        run(stage4, LAG4)
        run(stage5, LAG5)
        run(stage0, 0)

        @pl.when(it + 1 < PIECES)
        def _():
            zcopy(it + 1).wait_recv()
            spread(it + 1)

        @pl.when(it == 0)
        def _():
            project_send()

        @pl.when((it >= 2) & (it < 2 + PIECES))
        def _():
            @pl.when(it > 2)
            def _():
                zscopy(it - 2).wait_recv()

            for r in (2, 1, 3):
                sxcopy(it - 2, r).start()

        return carry

    lax.fori_loop(0, PIECES + LAG4, step, 0)

    for i in range(PIECES + LAG4 - LAG5, PIECES):
        stage5(i)
    lcc.wait_recv()
    low_ref[...] = (lowa[c] + lr[...].astype(F32)).astype(BF16)
    for k in range(1, PIECES):
        rarrive(k).wait_recv()
    for q in range(3):
        parts = []
        for e in range(EXPERTS):
            for part in (slice(q * MAIN, (q + 1) * MAIN), slice(3 * MAIN, BLOCK)):
                parts.append(rbk[0, e, part, :].astype(F32) + rbk[1, e, part, :].astype(F32))
        back = jnp.concatenate(parts, axis=0) * slotw_s[q]
        high = back.astype(BF16)
        rest = (back - high.astype(F32)).astype(BF16)
        mixed_ref[:, q * 256:(q + 1) * 256] = (dot_t(pick_s[q], high) + dot_t(pick_s[q], rest)).astype(BF16)

    lcc.wait_send()
    returned(PIECES - 1)


def moe(ids, route, tokens, cotangent, gate, up, down, projector):
    vm = lambda *shape: pltpu.VMEM(shape, BF16)
    vf = lambda *shape: pltpu.VMEM(shape, F32)
    sem = lambda *shape: pltpu.SemaphoreType.DMA(shape)
    n = PIECES
    scratch = [
        pltpu.VMEM((2, 64), jnp.int32), vf(2, 64), vm(64, 768), vm(64, 768),
        vm(4, 768, 256), vm(4, 768, 256), vm(2, 512, 768), vm(4, 768, 512),
        vm(3, 192, 64), vf(3, 192, 1), vm(3, ROWS, 192), vm(3, 192, ROWS),
        vm(4, BLOCK, 256), vm(n, 4, BLOCK, 256), vm(4, SLIM, 256), vm(3, SLIM, 256), vm(4, SLIM, 256), vm(4, n, SLIM, 256),
        vm(n, 2, ROWS, 256), vm(n, 2, ROWS, 256), vm(n, 2, ROWS, 256), vf(n, 2, ROWS, 256), vf(n, 2, ROWS, 256),
        vm(n, ROWS, 256), vm(n, ROWS, 256), vm(n, 2, ROWS, 256), vm(n, 2, ROWS, 256),
        vm(n, 4, 2, ROWS, 128), vm(n, 4, BLOCK, 256), vm(n, 4, BLOCK, 256), vm(n, BLOCK, 256), vm(2, 4, BLOCK, 256),
        vf(2, 512, 512), vm(512, 512), vm(512, 512),
        sem(10), sem(5), sem(5), sem(n), sem(n), sem(n), sem(n), sem(3), sem(3), sem(3), sem(3), sem(4, n), sem(4, n),
        sem(4, n), sem(4, n), sem(10, n), sem(10, n), sem(4, n), sem(4, n), sem(n), sem(n),
        pltpu.SemaphoreType.DMA, pltpu.SemaphoreType.DMA,
    ]
    vmem = pl.BlockSpec(memory_space=pltpu.VMEM)
    hbm = pl.BlockSpec(memory_space=pl.ANY)
    return pl.pallas_call(
        moe_kernel,
        out_shape=(
            jax.ShapeDtypeStruct((64, 768), BF16),
            jax.ShapeDtypeStruct((512, 512), BF16),
        ),
        in_specs=[hbm] * 8,
        out_specs=(vmem, vmem),
        scratch_shapes=scratch,
        compiler_params=pltpu.CompilerParams(
            collective_id=0, has_side_effects=True, vmem_limit_bytes=65000 * 1024
        ),
        cost_estimate=pl.CostEstimate(flops=8_000_000_000, bytes_accessed=6_000_000, transcendentals=300_000),
        name="moe",
    )(ids, route, tokens, cotangent, gate, up, down, projector)


def update_kernel(
    expert_ref, low_ref, first_ref, second_ref, proj_ref, mixed_ref, update_ref, new_first_ref, new_second_ref, out_ref
):
    out_ref[...] = mixed_ref[...]
    low = low_ref[...].astype(F32)
    new_first = 0.9 * first_ref[...] + 0.1 * low
    new_second = 0.999 * second_ref[...] + 0.001 * low * low
    new_first_ref[...] = new_first
    new_second_ref[...] = new_second
    bias_one = 1.0 - 0.9**10
    bias_two = 1.0 - 0.999**10
    direction = new_first / bias_one / (jnp.sqrt(new_second / bias_two) + 1e-08)
    high = direction.astype(BF16)
    rest = (direction - high.astype(F32)).astype(BF16)
    basis = proj_ref[0]
    dims = (((1,), (1,)), ((), ()))
    update_ref[...] = lax.dot_general(high, basis, dims, preferred_element_type=F32) + lax.dot_general(
        rest, basis, dims, preferred_element_type=F32
    )


def update_step(expert, low, first, second, projector, mixed):
    rows = 256
    return pl.pallas_call(
        update_kernel,
        out_shape=(
            jax.ShapeDtypeStruct((512, 768), F32),
            jax.ShapeDtypeStruct((512, 512), F32),
            jax.ShapeDtypeStruct((512, 512), F32),
            jax.ShapeDtypeStruct((64, 768), BF16),
        ),
        grid_spec=pltpu.PrefetchScalarGridSpec(
            num_scalar_prefetch=1,
            grid=(512 // rows,),
            in_specs=[
                pl.BlockSpec((rows, 512), lambda i, e: (i, 0)),
                pl.BlockSpec((rows, 512), lambda i, e: (i, 0)),
                pl.BlockSpec((rows, 512), lambda i, e: (i, 0)),
                pl.BlockSpec((1, 768, 512), lambda i, e: (e[0], 0, 0)),
                pl.BlockSpec((rows // 8, 768), lambda i, e: (i, 0)),
            ],
            out_specs=(
                pl.BlockSpec((rows, 768), lambda i, e: (i, 0)),
                pl.BlockSpec((rows, 512), lambda i, e: (i, 0)),
                pl.BlockSpec((rows, 512), lambda i, e: (i, 0)),
                pl.BlockSpec((rows // 8, 768), lambda i, e: (i, 0)),
            ),
        ),
        cost_estimate=pl.CostEstimate(flops=800_000_000, bytes_accessed=7_000_000, transcendentals=300_000),
        name="update",
    )(expert, low, first, second, projector, mixed)


def body(
    tokens,
    cotangent,
    expert_ids,
    route_weights,
    gate_weight,
    up_weight,
    down_weight,
    projector,
    first_moment,
    second_moment,
):
    mixed, low = moe(
        expert_ids.T, route_weights.T, tokens, cotangent, gate_weight, up_weight, down_weight, projector
    )
    expert = (lax.axis_index("fsdp") // 16).astype(jnp.int32).reshape(1)
    update, new_first, new_second, mixed = update_step(
        expert, low, first_moment, second_moment, projector, mixed
    )
    return mixed, update, new_first, new_second


def solution(mesh):
    in_specs = (
        P("fsdp", "tp"),
        P("fsdp", "tp"),
        P("fsdp", None),
        P("fsdp", None),
        P("tp", "fsdp"),
        P("tp", "fsdp"),
        P("fsdp", "tp"),
        P(None, "tp", None),
        P("fsdp", None),
        P("fsdp", None),
    )
    out_specs = (P("fsdp", "tp"), P("fsdp", "tp"), P("fsdp", None), P("fsdp", None))
    return jax.shard_map(body, mesh=mesh, in_specs=in_specs, out_specs=out_specs, check_vma=False)
```
